128 devices in a mesh: blk: 16 (over x, z_lo, core), uly: 8 (over z_hi, y).
Axes of the slice: x: 4, y: 4, z: 4 (z_hi: 2, z_lo: 2; z = z_hi * 2 + z_lo), core: 2. Of those that a mesh axis runs over, the one named last changes fastest.
Arguments:
- activations: bfloat16 [12288, 4096], P(('blk', 'uly')), may hold values from -64 to 64
- input_norm_gain: float32 [4096], replicated, may hold values from 0.5 to 2
- query_weight: bfloat16 [4096, 4096], P(None, 'uly'), may hold values from -3 to 3
- key_weight: bfloat16 [4096, 1024], P(None, 'uly'), may hold values from -3 to 3
- value_weight: bfloat16 [4096, 1024], P(None, 'uly'), may hold values from -0.09375 to 0.09375
- output_weight: bfloat16 [4096, 4096], P('uly'), may hold values from -1 to 1
- adapter_down_maps: bfloat16 [4096, 384], replicated, may hold values from -0.09375 to 0.09375
- query_up_maps: bfloat16 [128, 4096], P(None, 'uly'), may hold values from -0.375 to 0.375
- key_up_maps: bfloat16 [128, 1024], P(None, 'uly'), may hold values from -0.375 to 0.375
- value_up_maps: bfloat16 [128, 1024], P(None, 'uly'), may hold values from -0.375 to 0.375
- output_down_maps: bfloat16 [4096, 128], P('uly'), may hold values from -0.5 to 0.5
- output_up_maps: bfloat16 [128, 4096], replicated, may hold values from -1.5 to 1.5
- segment_index: int32 [12288], replicated, may hold values from 0 to 3, never falling along the last dimension, each value on 1 to 9216 neighbouring positions
- segment_adapter: int32 [4], replicated, may hold values from 0 to 7
Outputs:
- attn_out: bfloat16 [12288, 4096], P(('blk', 'uly'))
The draws below stay inside these ranges and needn't reach their ends.
Inputs may be any that keep to these rules, and one draw needn't show every extreme that they name: `segment_index`: never falling along the sequence; each of the 4 segments covers 1 to 9216 tokens, and one covers exactly that many. `segment_adapter`: one adapter per segment; segments may share one.
All inputs are finite; a program needn't handle non-finite values.
Results may differ from the reference program's by a relative error of at most 0.019.
The reference program's roundings to bfloat16 on the way count: a program that leaves them out, or rounds other values in their place, can miss the bound.
Values may be sent and summed in bfloat16 or wider, within the bound.
No kernel may reach another device: no remote copies, remote signals or barrier semaphores. Data moves between devices by JAX's collectives and lax.ppermute only.
A program may use at most 192 MiB of HBM per device.

```python
import math
import jax
import jax.numpy as jnp
import numpy as np
from jax import lax

MODEL_WIDTH = 4096
QUERY_HEADS = 32
KEY_VALUE_HEADS = 8
HEAD_SIZE = 128
ADAPTER_RANK = 16
ADAPTER_COUNT = 8
SEGS = 4
TOKEN_COUNT = 12288


def base_query(key):
    return jnp.clip(jax.random.normal(key, (MODEL_WIDTH, QUERY_HEADS * HEAD_SIZE), jnp.float32), -6.0, 6.0)


def draw_query_weight(key, part):
    base_output = base_query(key)
    factor = 1.4
    return jnp.clip(base_output * factor / math.sqrt(MODEL_WIDTH), -3.0, 3.0).astype(jnp.bfloat16)


def draw_key_weight(key, part):
    key = jax.random.fold_in(key, 12)
    random_noise = jnp.clip(jax.random.normal(key, (MODEL_WIDTH, KEY_VALUE_HEADS * HEAD_SIZE), jnp.float32), -6.0, 6.0)
    mixed_heads = 1.4 * random_noise
    return jnp.clip(mixed_heads / math.sqrt(MODEL_WIDTH), -3.0, 3.0).astype(jnp.bfloat16)


def draw_activations(key, part):
    key = jax.random.fold_in(key, 13)
    first = jax.random.fold_in(key, 0)
    base_output = jax.random.normal(first, (TOKEN_COUNT, MODEL_WIDTH), jnp.float32)
    values = base_output
    return jnp.clip(values, -64.0, 64.0).astype(jnp.bfloat16)


def set_ends(result, key, least, high):
    dims = result.shape
    place = [jax.random.randint(jax.random.fold_in(key, axis), (), 0, dims[axis]) for axis in range(len(dims))]
    result = result.at[tuple(place)].set(least)
    longest = dims.index(max(dims))
    place[longest] = (place[longest] + 1) % dims[longest]
    return result.at[tuple(place)].set(high)


def block_levels(key, dims, pieces, low, high):
    loudness, own = 1.0, jax.random.fold_in(key, 6)
    for position, parts in pieces:
        heights = jnp.exp(jax.random.uniform(jax.random.fold_in(own, position), (parts,), jnp.float32, low / len(pieces), high / len(pieces)))
        loudness = loudness * jnp.repeat(heights, dims[position] // parts).reshape([-1 if axis == position else 1 for axis in range(len(dims))])
    return loudness


def profile(count, total, reach, slope):
    portions = [(1 << 20) // math.isqrt(grade ** slope) + 1 for grade in range(2, count + 1)]
    spare, given = total - reach - (count - 1), [1] * (count - 1)
    while spare > 0:
        free = [i for i in range(count - 1) if given[i] < reach]
        mass, remaining = sum([portions[i] for i in free]), spare
        for i in free:
            more = min(reach - given[i], max(1, remaining * portions[i] // mass), spare)
            given[i] = given[i] + more
            spare = spare - more
    return np.array([reach] + given)


def uneven(rng, count, total, bound, lean):
    if count == 2:
        one = jax.random.randint(rng, (), max(1, total - bound), min(bound, total - 1) + 1)
        return jnp.stack([one, total - one])
    sizes = jnp.asarray(profile(count, total, bound, lean), jnp.int32)
    couples = (count - 1) // 2
    donor, taker = sizes[1:1 + 2 * couples:2], sizes[2:2 + 2 * couples:2]
    margin = jnp.minimum(donor - 1, bound - taker)
    passed = jax.random.randint(jax.random.fold_in(rng, 1), (couples,), 0, 1 << 20) % (margin + 1)
    sizes = sizes.at[1:1 + 2 * couples:2].set(donor - passed).at[2:2 + 2 * couples:2].set(taker + passed)
    return sizes[jax.random.permutation(jax.random.fold_in(rng, 2), count)]


def noise(rng, shape, spread, most, cuts=(), held_as=jnp.bfloat16):
    gain = block_levels(rng, shape, cuts, -0.22, 0.18) if cuts else 1.0
    entries = jax.random.normal(rng, shape, jnp.float32) * spread * gain
    return jnp.minimum(jnp.maximum(entries, -most), most).astype(held_as)


def setup_inputs(seed: int = 0) -> dict:
    streams_of = jax.random.split(jax.random.key(seed), 15)
    activations = draw_activations(jax.random.fold_in(streams_of[14], 71), 0)
    input_norm_gain = jnp.clip(jnp.exp(jax.random.uniform(streams_of[1], (MODEL_WIDTH,), jnp.float32, math.log(0.5), math.log(2.0))), 0.5, 2.0)
    query_weight = draw_query_weight(jax.random.fold_in(streams_of[14], 71), 0)
    key_weight = draw_key_weight(jax.random.fold_in(streams_of[14], 71), 0)
    value_weight = noise(streams_of[4], (MODEL_WIDTH, KEY_VALUE_HEADS * HEAD_SIZE), MODEL_WIDTH ** -0.5, 0.09375, ((1, 8),))
    output_weight = noise(streams_of[5], (QUERY_HEADS * HEAD_SIZE, MODEL_WIDTH), (HEAD_SIZE // 4) ** -0.5, 1.0, ((0, 8),))
    adapter_down_maps = noise(streams_of[6], (MODEL_WIDTH, 3 * ADAPTER_COUNT * ADAPTER_RANK), MODEL_WIDTH ** -0.5, 0.09375)
    query_up_maps = noise(streams_of[7], (ADAPTER_COUNT * ADAPTER_RANK, QUERY_HEADS * HEAD_SIZE), (16 * ADAPTER_RANK) ** -0.5, 0.375, ((1, 8),))
    key_up_maps = noise(streams_of[8], (ADAPTER_COUNT * ADAPTER_RANK, KEY_VALUE_HEADS * HEAD_SIZE), (16 * ADAPTER_RANK) ** -0.5, 0.375, ((1, 8),))
    value_up_maps = noise(streams_of[9], (ADAPTER_COUNT * ADAPTER_RANK, KEY_VALUE_HEADS * HEAD_SIZE), (16 * ADAPTER_RANK) ** -0.5, 0.375, ((1, 8),))
    output_down_maps = noise(streams_of[10], (QUERY_HEADS * HEAD_SIZE, ADAPTER_COUNT * ADAPTER_RANK), HEAD_SIZE ** -0.5, 0.5, ((0, 8),))
    output_up_maps = noise(streams_of[11], (ADAPTER_COUNT * ADAPTER_RANK, MODEL_WIDTH), ADAPTER_RANK ** -0.5, 1.5)
    segment_index = jnp.searchsorted(jnp.cumsum(uneven(streams_of[12], SEGS, TOKEN_COUNT, TOKEN_COUNT * 3 // 4, 0)), jnp.arange(TOKEN_COUNT), side="right").astype(jnp.int32)
    segment_adapter = set_ends(jax.random.randint(streams_of[13], (SEGS,), 0, ADAPTER_COUNT), jax.random.fold_in(streams_of[13], 1), 0, ADAPTER_COUNT - 1).astype(jnp.int32)
    return dict(activations=activations, input_norm_gain=input_norm_gain, query_weight=query_weight, key_weight=key_weight, value_weight=value_weight, output_weight=output_weight, adapter_down_maps=adapter_down_maps, query_up_maps=query_up_maps, key_up_maps=key_up_maps, value_up_maps=value_up_maps, output_down_maps=output_down_maps, output_up_maps=output_up_maps, segment_index=segment_index, segment_adapter=segment_adapter)


eps_norm = 1e-05
adapter_scale = 2.0

def tenant_rows(seg_rows, segment_adapter):
    match = seg_rows[:, None] == jnp.arange(segment_adapter.shape[0], dtype=jnp.int32)[None, :]
    return lax.optimization_barrier(jnp.sum(jnp.where(match, segment_adapter[None, :], 0), axis=1)).astype(jnp.int32)

def normalize(activations, input_norm_gain):
    values = activations.astype(jnp.float32)
    power = lax.optimization_barrier(jnp.mean(values * values, axis=1, keepdims=True))
    return (values * lax.rsqrt(power + eps_norm) * input_norm_gain[None, :]).astype(jnp.bfloat16)

def tenant_adapter_mask(tenant_index, hidden_width):
    columns = jnp.arange(hidden_width, dtype=jnp.int32) // ADAPTER_RANK % ADAPTER_COUNT
    return columns[None, :] == tenant_index[:, None]

def attend(query_rows, key_matrix_rows, value_matrix_rows, segment_index):
    query_group = QUERY_HEADS // KEY_VALUE_HEADS
    token_block = math.gcd(TOKEN_COUNT, 256)
    score_scale = 1.0 / math.sqrt(HEAD_SIZE)
    positions = jnp.arange(TOKEN_COUNT, dtype=jnp.int32)
    every_key = key_matrix_rows.astype(jnp.float32).reshape(TOKEN_COUNT, KEY_VALUE_HEADS, HEAD_SIZE)
    every_value = value_matrix_rows.astype(jnp.float32).reshape(TOKEN_COUNT, KEY_VALUE_HEADS, HEAD_SIZE)
    query_matrix = query_rows.reshape(TOKEN_COUNT // token_block, token_block, KEY_VALUE_HEADS, query_group, HEAD_SIZE)
    starts = jnp.arange(TOKEN_COUNT // token_block, dtype=jnp.int32) * token_block

    def one_block(input_rows):
        rows_in, start = input_rows
        query_pos = start + jnp.arange(token_block, dtype=jnp.int32)
        query_seg = lax.dynamic_slice_in_dim(segment_index, start, token_block)
        allowed = (positions[None, :] <= query_pos[:, None]) & (segment_index[None, :] == query_seg[:, None])
        allowed = allowed[:, None, None, :]
        scores = jnp.einsum('rkgd,nkd->rkgn', rows_in.astype(jnp.float32), every_key) * score_scale
        peak = lax.optimization_barrier(jnp.max(jnp.where(allowed, scores, -1e+30), axis=3, keepdims=True))
        weights = jnp.where(allowed, jnp.exp(scores - peak), 0.0)
        total = lax.optimization_barrier(jnp.sum(weights, axis=3))
        rounded = lax.optimization_barrier(weights.astype(jnp.bfloat16)).astype(jnp.float32)
        summed = jnp.einsum('rkgn,nkd->rkgd', rounded, every_value)
        return (summed / total[..., None]).reshape(token_block, QUERY_HEADS * HEAD_SIZE).astype(jnp.bfloat16)
    return lax.map(one_block, (query_matrix, starts)).reshape(TOKEN_COUNT, QUERY_HEADS * HEAD_SIZE)

def reference(activations, input_norm_gain, query_weight, key_weight, value_weight, output_weight, adapter_down_maps, query_up_maps, key_up_maps, value_up_maps, output_down_maps, output_up_maps, segment_index, segment_adapter):
    hidden_width = ADAPTER_COUNT * ADAPTER_RANK
    normed_input = normalize(activations, input_norm_gain)
    tenant_index = tenant_rows(segment_index, segment_adapter)
    lowered_rows = jnp.where(tenant_adapter_mask(tenant_index, 3 * hidden_width), jnp.dot(normed_input, adapter_down_maps, preferred_element_type=jnp.float32), 0.0).astype(jnp.bfloat16)
    query_rows = (jnp.dot(normed_input, query_weight, preferred_element_type=jnp.float32) + adapter_scale * jnp.dot(lowered_rows[:, :hidden_width], query_up_maps, preferred_element_type=jnp.float32)).astype(jnp.bfloat16)
    key_matrix_rows = (jnp.dot(normed_input, key_weight, preferred_element_type=jnp.float32) + adapter_scale * jnp.dot(lowered_rows[:, hidden_width:2 * hidden_width], key_up_maps, preferred_element_type=jnp.float32)).astype(jnp.bfloat16)
    value_matrix_rows = (jnp.dot(normed_input, value_weight, preferred_element_type=jnp.float32) + adapter_scale * jnp.dot(lowered_rows[:, 2 * hidden_width:], value_up_maps, preferred_element_type=jnp.float32)).astype(jnp.bfloat16)
    mixed_heads = attend(query_rows, key_matrix_rows, value_matrix_rows, segment_index)
    rank_rows = jnp.where(tenant_adapter_mask(tenant_index, hidden_width), jnp.dot(mixed_heads, output_down_maps, preferred_element_type=jnp.float32), 0.0)
    block_result = jnp.dot(mixed_heads, output_weight, preferred_element_type=jnp.float32) + adapter_scale * jnp.dot(rank_rows, output_up_maps.astype(jnp.float32), precision=lax.Precision.HIGHEST)
    return block_result.astype(jnp.bfloat16)
```

```python
import functools
import math

import jax
import jax.numpy as jnp
from jax import lax
from jax.experimental import pallas as pl
from jax.experimental.pallas import tpu as pltpu
from jax.sharding import PartitionSpec as P

HEAD_SIZE = 128
ADAPTER_RANK = 16
ADAPTER_COUNT = 8
GROUP = 4
PIECE = 96
HALF = 384
BLOCK = 768
BLOCKS = 16
EPS_NORM = 1e-05
ADAPTER_SCALE = 2.0
MASKED = -1e30
LEAST = -1e20
EXP2_SCALE = math.log2(math.e) / math.sqrt(HEAD_SIZE)
MIB = 2**20

INFO = 24


def pos_of(info, bases, width, axis):
    shape = (width * len(bases), 1) if axis == 0 else (1, width * len(bases))
    index = lax.broadcasted_iota(jnp.int32, shape, axis)
    pos = index + info[bases[0]]
    for i, base in enumerate(bases[1:], 1):
        pos = jnp.where(index >= i * width, index + (info[base] - i * width), pos)
    return pos


def start_of(info, pos):
    start = jnp.zeros_like(pos)
    for s in range(8, 11):
        start = jnp.where(pos >= info[s], info[s], start)
    return start


def tenant_of(info, pos):
    tenant = jnp.zeros_like(pos) + info[11]
    for s in range(3):
        tenant = jnp.where(pos >= info[8 + s], info[12 + s], tenant)
    return tenant


def keep_columns(info, bases, columns):
    tenant = tenant_of(info, pos_of(info, bases, PIECE, 0))
    column = lax.broadcasted_iota(jnp.int32, (len(bases) * PIECE, columns), 1)
    return (column // ADAPTER_RANK) % ADAPTER_COUNT == tenant


def project_kernel(info, *refs, bases, parts):
    rows = refs[:parts]
    wq, wk, wv, down, q_up, k_up, v_up, q_out, kv_out, acc = refs[parts:]
    step = pl.program_id(0)
    x = jnp.concatenate([r[...] for r in rows], axis=0)
    nq, nk = wq.shape[1], wk.shape[1]
    spans = ((0, nq, wq), (nq, nk, wk), (nq + nk, nk, wv), (nq + 2 * nk, down.shape[1], down))

    @pl.when(step == 0)
    def _():
        for at, width, w in spans:
            acc[:, at : at + width] = jnp.dot(x, w[...], preferred_element_type=jnp.float32)

    @pl.when(step > 0)
    def _():
        for at, width, w in spans:
            acc[:, at : at + width] += jnp.dot(x, w[...], preferred_element_type=jnp.float32)

    @pl.when(step == pl.num_programs(0) - 1)
    def _():
        hidden = ADAPTER_COUNT * ADAPTER_RANK
        low = acc[:, nq + 2 * nk :]
        low = jnp.where(keep_columns(info, bases, 3 * hidden), low, 0.0).astype(jnp.bfloat16)

        def with_adapter(at, width, i, up):
            return (
                acc[:, at : at + width]
                + ADAPTER_SCALE
                * jnp.dot(
                    low[:, i * hidden : (i + 1) * hidden],
                    up[...],
                    preferred_element_type=jnp.float32,
                )
            ).astype(jnp.bfloat16)

        q_out[...] = with_adapter(0, nq, 0, q_up)
        kv_out[:, :nk] = with_adapter(nq, nk, 1, k_up)
        kv_out[:, nk:] = with_adapter(nq + nk, nk, 2, v_up)


def project(info, rows, bases, wq, wk, wv, down, q_up, k_up, v_up):
    depth, nq, nk = wq.shape[0], wq.shape[1], wk.shape[1]
    count = sum(r.shape[0] for r in rows)
    chunk = 1024
    along = lambda a: pl.BlockSpec((a.shape[0], chunk), lambda i, s: (0, i))
    down_ = lambda a: pl.BlockSpec((chunk, a.shape[1]), lambda i, s: (i, 0))
    whole = lambda a: pl.BlockSpec(a.shape, lambda i, s: (0, 0))
    wide = nq + 2 * nk + down.shape[1]
    return pl.pallas_call(
        functools.partial(project_kernel, bases=bases, parts=len(rows)),
        out_shape=(
            jax.ShapeDtypeStruct((count, nq), jnp.bfloat16),
            jax.ShapeDtypeStruct((count, 2 * nk), jnp.bfloat16),
        ),
        grid_spec=pltpu.PrefetchScalarGridSpec(
            num_scalar_prefetch=1,
            grid=(depth // chunk,),
            in_specs=[along(r) for r in rows]
            + [down_(w) for w in (wq, wk, wv, down)]
            + [whole(u) for u in (q_up, k_up, v_up)],
            out_specs=(
                pl.BlockSpec((count, nq), lambda i, s: (0, 0)),
                pl.BlockSpec((count, 2 * nk), lambda i, s: (0, 0)),
            ),
            scratch_shapes=[pltpu.VMEM((count, wide), jnp.float32)],
        ),
        compiler_params=pltpu.CompilerParams(vmem_limit_bytes=48 * MIB),
        cost_estimate=pl.CostEstimate(
            flops=2 * count * depth * wide,
            bytes_accessed=2 * depth * (wide + count),
            transcendentals=0,
        ),
    )(info, *rows, wq, wk, wv, down, q_up, k_up, v_up)


def attend_kernel(info, q1, q2, kv1, kv2, out, kv, sem, qt, acc, peak, held, held_peak, *, own, tile, width):
    copies = []
    for part, pieces in ((kv1, ((0, 15), (1, 16), (2, 17), (3, 19))), (kv2, ((0, 18), (1, 20), (2, 21), (3, 22)))):
        for i, place in pieces:
            to = pl.ds(pl.multiple_of(info[place] * PIECE, PIECE), PIECE)
            if place < 19:
                copies.append((part.at[:, :, :, i], kv.at[:, :, :, to]))
            else:
                for z in range(2):
                    copies.append((part.at[:, z, :, i], kv.at[:, 1 - z, :, to]))
    started = []
    for n, (source, target) in enumerate(copies):
        started.append(pltpu.make_async_copy(source, target, sem.at[n]))
        started[-1].start()
    if own:
        groups = ((q1, 0, 0, 3), (q2, 0, 3, 1))
        bases = (0, 1, 2, 3)
    else:
        groups = ((q1, 3, 0, 1), (q2, 1, 1, 3))
        bases = (4, 5, 6, 7)
    q = jnp.concatenate([r[a * PIECE : (a + n) * PIECE] for r, a, _, n in groups], axis=0)
    for h in range(GROUP):
        qt[:, h * HALF : (h + 1) * HALF] = q[:, h * HEAD_SIZE : (h + 1) * HEAD_SIZE].T
    total = GROUP * HALF
    peak[...] = jnp.full((1, total), LEAST, jnp.float32)
    acc[...] = jnp.zeros((HEAD_SIZE + 8, total), jnp.float32)
    pos = pos_of(info, bases, PIECE, 1)
    low = start_of(info, pos)
    pos = jnp.concatenate([pos] * GROUP, axis=1)
    low = jnp.concatenate([low] * GROUP, axis=1)
    first = info[bases[0]]
    for b in bases[1:]:
        first = jnp.minimum(first, info[b])
    last = first + (HALF - 1)
    n0 = start_of(info, first) // tile
    n3 = last // tile + 1
    m1 = jnp.clip((start_of(info, last) + tile - 1) // tile, n0, n3)
    m2 = jnp.clip(first // tile, m1, n3)
    ahead = m1 - n0
    for c in started:
        c.wait()

    def of_tile(j, at):
        return kv[j // 4, (j // 2) % 2, j % 2, :, at : at + HEAD_SIZE]

    def step(now, later, masked):
        if later is not None:
            keys = of_tile(later, 0)
        if now is not None:
            values = jnp.concatenate(
                [of_tile(now, HEAD_SIZE).T, jnp.ones((8, tile), jnp.bfloat16)], axis=0
            )
        for c in range(0, total, width):
            at = slice(c, c + width)
            if now is not None:
                old = peak[:, at]
                fresh = jnp.maximum(old, held_peak[:, at])
                weights = jnp.exp2((held[:, at] - fresh) * EXP2_SCALE).astype(jnp.bfloat16)
                decay = jnp.exp2((old - fresh) * EXP2_SCALE)
                peak[:, at] = fresh
            if later is not None:
                scores = jnp.dot(keys, qt[:, at], preferred_element_type=jnp.float32)
                if masked:
                    key_pos = later * tile + lax.broadcasted_iota(jnp.int32, (tile, width), 0)
                    allowed = (key_pos <= pos[:, at]) & (key_pos >= low[:, at])
                    scores = jnp.where(allowed, scores, MASKED)
                held[:, at] = scores
                held_peak[:, at] = jnp.max(scores, axis=0, keepdims=True)
            if now is not None:
                acc[:, at] = acc[:, at] * decay + jnp.dot(
                    values, weights, preferred_element_type=jnp.float32
                )

    def masked_tile(i):
        return jnp.where(i < ahead, n0 + i, m2 + i - ahead)

    def masked_step(i, now):
        step(now, masked_tile(i), True)
        return masked_tile(i)

    def plain_step(j, now):
        step(now, j, False)
        return j

    step(None, masked_tile(0), True)
    now = lax.fori_loop(1, ahead + n3 - m2, masked_step, masked_tile(0))
    now = lax.fori_loop(m1, m2, plain_step, now)
    step(now, None, False)
    for h in range(GROUP):
        at = slice(h * HALF, (h + 1) * HALF)
        mixed = acc[:HEAD_SIZE, at] / acc[HEAD_SIZE : HEAD_SIZE + 1, at]
        out[:, h * HEAD_SIZE : (h + 1) * HEAD_SIZE] = mixed.T.astype(jnp.bfloat16)


def attend(info, q1, q2, kv1, kv2, own):
    total = GROUP * HALF
    tile, width = BLOCK, 512
    flat = lambda a: pl.BlockSpec(a.shape, lambda i, s: (0, 0))
    anywhere = pl.BlockSpec(memory_space=pl.ANY)
    return pl.pallas_call(
        functools.partial(attend_kernel, own=own, tile=tile, width=width),
        out_shape=jax.ShapeDtypeStruct((HALF, GROUP * HEAD_SIZE), jnp.bfloat16),
        grid_spec=pltpu.PrefetchScalarGridSpec(
            num_scalar_prefetch=1,
            grid=(1,),
            in_specs=[flat(q1), flat(q2), anywhere, anywhere],
            out_specs=pl.BlockSpec((HALF, GROUP * HEAD_SIZE), lambda i, s: (0, 0)),
            scratch_shapes=[
                pltpu.VMEM((4, 2, 2, BLOCK, 2 * HEAD_SIZE), jnp.bfloat16),
                pltpu.SemaphoreType.DMA((12,)),
                pltpu.VMEM((HEAD_SIZE, total), jnp.bfloat16),
                pltpu.VMEM((HEAD_SIZE + 8, total), jnp.float32),
                pltpu.VMEM((1, total), jnp.float32),
                pltpu.VMEM((tile, total), jnp.float32),
                pltpu.VMEM((1, total), jnp.float32),
            ],
        ),
        compiler_params=pltpu.CompilerParams(vmem_limit_bytes=48 * MIB),
        cost_estimate=pl.CostEstimate(
            flops=2 * 2 * total * BLOCKS * BLOCK * HEAD_SIZE,
            bytes_accessed=8 * MIB,
            transcendentals=total * BLOCKS * BLOCK,
        ),
    )(info, q1, q2, kv1, kv2)


def output_kernel(info, mixed, weight, down, up, *rest, bases):
    *outs, high, rest_low = rest

    @pl.when(pl.program_id(0) == 0)
    def _():
        lows = jnp.dot(mixed[...], down[...], preferred_element_type=jnp.float32)
        lows = jnp.where(keep_columns(info, bases, lows.shape[1]), ADAPTER_SCALE * lows, 0.0)
        top = lows.astype(jnp.bfloat16)
        high[...] = top
        rest_low[...] = (lows - top.astype(jnp.float32)).astype(jnp.bfloat16)

    result = jnp.dot(mixed[...], weight[...], preferred_element_type=jnp.float32)
    result += jnp.dot(high[...], up[...], preferred_element_type=jnp.float32)
    result += jnp.dot(rest_low[...], up[...], preferred_element_type=jnp.float32)
    result = result.astype(jnp.bfloat16)
    for i, out in enumerate(outs):
        out[...] = result[i * PIECE : (i + 1) * PIECE]


def output(info, mixed, weight, down, up, bases):
    features = weight.shape[1]
    chunk = 512
    whole = lambda a: pl.BlockSpec(a.shape, lambda i, s: (0, 0))
    across = lambda n: pl.BlockSpec((n, chunk), lambda i, s: (0, i))
    return pl.pallas_call(
        functools.partial(output_kernel, bases=bases),
        out_shape=(jax.ShapeDtypeStruct((PIECE, features), jnp.bfloat16),) * 4,
        grid_spec=pltpu.PrefetchScalarGridSpec(
            num_scalar_prefetch=1,
            grid=(features // chunk,),
            in_specs=[whole(mixed), across(weight.shape[0]), whole(down), across(up.shape[0])],
            out_specs=(across(PIECE),) * 4,
            scratch_shapes=[pltpu.VMEM((HALF, down.shape[1]), jnp.bfloat16)] * 2,
        ),
        compiler_params=pltpu.CompilerParams(vmem_limit_bytes=48 * MIB),
        cost_estimate=pl.CostEstimate(
            flops=2 * HALF * (weight.shape[0] + 2 * up.shape[0]) * features,
            bytes_accessed=2 * features * (weight.shape[0] + up.shape[0] + HALF),
            transcendentals=0,
        ),
    )(info, mixed, weight, down, up)


def normalize(activations, input_norm_gain):
    values = activations.astype(jnp.float32)
    power = jnp.mean(values * values, axis=1, keepdims=True)
    return (values * lax.rsqrt(power + EPS_NORM) * input_norm_gain[None, :]).astype(jnp.bfloat16)


def along_y(rows, hop):
    return lax.ppermute(
        rows, "uly", [(z * 4 + y, z * 4 + (y + hop) % 4) for z in range(2) for y in range(4)]
    )


def across_z(rows):
    pairs = [(b * 8 + u, (b ^ 2) * 8 + (u ^ 4)) for b in range(16) for u in range(8)]
    return lax.ppermute(rows, ("blk", "uly"), pairs)


def plan(segment_index, segment_adapter):
    block, head = lax.axis_index("blk"), lax.axis_index("uly")
    z, y = head // 4, head % 4
    ys = [y, (y + 3) % 4, (y + 1) % 4, (y + 2) % 4]
    here = [z * 4 + p for p in ys]
    there = [(1 - z) * 4 + p for p in ys]
    firsts = [block * BLOCK + p * PIECE for p in here]
    firsts += [(block ^ 2) * BLOCK + p * PIECE for p in there]
    ends = jnp.sum(
        segment_index[None, :] < jnp.arange(1, 4, dtype=jnp.int32)[:, None], axis=1, dtype=jnp.int32
    )
    return jnp.concatenate(
        [
            jnp.stack(firsts).astype(jnp.int32),
            ends,
            segment_adapter,
            jnp.stack(here + there).astype(jnp.int32),
            jnp.zeros((INFO - 23,), jnp.int32),
        ]
    )


def added(*terms):
    return sum(t.astype(jnp.float32) for t in terms).astype(jnp.bfloat16)


def shards(
    activations,
    input_norm_gain,
    query_weight,
    key_weight,
    value_weight,
    output_weight,
    adapter_down_maps,
    query_up_maps,
    key_up_maps,
    value_up_maps,
    output_down_maps,
    output_up_maps,
    segment_index,
    segment_adapter,
):
    info = plan(segment_index, segment_adapter)
    weights = (
        query_weight,
        key_weight,
        value_weight,
        adapter_down_maps,
        query_up_maps,
        key_up_maps,
        value_up_maps,
    )
    mid = PIECE // 2
    own = normalize(activations, input_norm_gain)
    own_m, own_p, other = along_y(own, 1), along_y(own, -1), across_z(own)
    far_top, far_end = along_y(own_m[:mid], 1), along_y(own_p[mid:], -1)
    other_m, other_p = along_y(other, 1), along_y(other, -1)
    other_far = across_z(jnp.concatenate([far_top, far_end], axis=0))

    def gathered(kv):
        return lax.all_gather(kv, "blk", axis=0).reshape(4, 2, 2, 4, PIECE, 2 * HEAD_SIZE)

    q1, kv1 = project(info, [own, own_m, own_p, other], (0, 1, 2, 4), *weights)
    kv1 = gathered(kv1)
    q2, kv2 = project(
        info, [far_top, far_end, other_m, other_p, other_far], (3, 5, 6, 7), *weights
    )
    kv2 = gathered(kv2)

    out_weights = (output_weight, output_down_maps, output_up_maps)
    mixed = attend(info, q1, q2, kv1, kv2, False)
    b0, bm, bp, bf = output(info, mixed, *out_weights, (4, 5, 6, 7))
    for_far = across_z(bf)
    from_m, from_p = along_y(bp, 1), along_y(bm, -1)
    mixed = attend(info, q1, q2, kv1, kv2, True)
    a0, am, ap, af = output(info, mixed, *out_weights, (0, 1, 2, 3))
    for_other = across_z(added(b0, from_m, from_p))
    far = added(af, for_far)
    top, end = along_y(far[:mid], 1), along_y(far[mid:], -1)
    to_p = jnp.concatenate([added(ap[:mid], top), ap[mid:]], axis=0)
    to_m = jnp.concatenate([am[:mid], added(am[mid:], end)], axis=0)
    return added(a0, along_y(to_p, 1), along_y(to_m, -1), for_other)


def solution(mesh):
    return jax.shard_map(
        shards,
        mesh=mesh,
        in_specs=(
            P(("blk", "uly"), None),
            P(),
            P(None, "uly"),
            P(None, "uly"),
            P(None, "uly"),
            P("uly", None),
            P(),
            P(None, "uly"),
            P(None, "uly"),
            P(None, "uly"),
            P("uly", None),
            P(),
            P(),
            P(),
        ),
        out_specs=P(("blk", "uly"), None),
        check_vma=False,
    )
```

```python
import functools
import math

import jax
import jax.numpy as jnp
from jax import lax
from jax.experimental import pallas as pl
from jax.experimental.pallas import tpu as pltpu
from jax.sharding import PartitionSpec as P

HEAD_SIZE = 128
ADAPTER_RANK = 16
ADAPTER_COUNT = 8
GROUP = 4
PIECE = 96
HALF = 384
BLOCK = 768
BLOCKS = 16
OTHER = 2
EPS_NORM = 1e-05
ADAPTER_SCALE = 2.0
MASKED = -1e30
LEAST = -1e20
EXP2_SCALE = math.log2(math.e) / math.sqrt(HEAD_SIZE)
MIB = 2**20
HELD = pl.BlockSpec(memory_space=pltpu.VMEM)
CHUNKS = (0, 1, 2, 4, 3, 5, 6, 7)
WIDTH = 512

INFO = 26


def pos_of(info, bases, width, axis):
    shape = (width * len(bases), 1) if axis == 0 else (1, width * len(bases))
    index = lax.broadcasted_iota(jnp.int32, shape, axis)
    pos = index + info[bases[0]]
    for i, base in enumerate(bases[1:], 1):
        pos = jnp.where(index >= i * width, index + (info[base] - i * width), pos)
    return pos


def start_of(info, pos):
    start = jnp.zeros_like(pos)
    for s in range(8, 11):
        start = jnp.where(pos >= info[s], info[s], start)
    return start


def tenant_of(info, pos):
    tenant = jnp.zeros_like(pos) + info[11]
    for s in range(3):
        tenant = jnp.where(pos >= info[8 + s], info[12 + s], tenant)
    return tenant


def keep_columns(info, bases, columns):
    tenant = tenant_of(info, pos_of(info, bases, PIECE, 0))
    column = lax.broadcasted_iota(jnp.int32, (len(bases) * PIECE, columns), 1)
    return (column // ADAPTER_RANK) % ADAPTER_COUNT == tenant


def project_kernel(info, *refs, bases, parts):
    rows = refs[:parts]
    wq, wk, wv, down, q_up, k_up, v_up, q_out, kv_out, acc = refs[parts:]
    step = pl.program_id(0)
    chunk = wq.shape[0]
    columns = pl.ds(pl.multiple_of(step * chunk, chunk), chunk)
    x = jnp.concatenate([r[:, columns] for r in rows], axis=0)
    nq, nk = wq.shape[1], wk.shape[1]
    spans = ((0, nq, wq), (nq, nk, wk), (nq + nk, nk, wv), (nq + 2 * nk, down.shape[1], down))

    @pl.when(step == 0)
    def _():
        for at, width, w in spans:
            acc[:, at : at + width] = jnp.dot(x, w[...], preferred_element_type=jnp.float32)

    @pl.when(step > 0)
    def _():
        for at, width, w in spans:
            acc[:, at : at + width] += jnp.dot(x, w[...], preferred_element_type=jnp.float32)

    @pl.when(step == pl.num_programs(0) - 1)
    def _():
        hidden = ADAPTER_COUNT * ADAPTER_RANK
        low = acc[:, nq + 2 * nk :]
        low = jnp.where(keep_columns(info, bases, 3 * hidden), low, 0.0).astype(jnp.bfloat16)

        def with_adapter(at, width, i, up):
            return (
                acc[:, at : at + width]
                + ADAPTER_SCALE
                * jnp.dot(
                    low[:, i * hidden : (i + 1) * hidden],
                    up[...],
                    preferred_element_type=jnp.float32,
                )
            ).astype(jnp.bfloat16)

        q_out[...] = with_adapter(0, nq, 0, q_up)
        kv_out[:, :nk] = with_adapter(nq, nk, 1, k_up)
        kv_out[:, nk:] = with_adapter(nq + nk, nk, 2, v_up)


def project(info, rows, bases, wq, wk, wv, down, q_up, k_up, v_up):
    depth, nq, nk = wq.shape[0], wq.shape[1], wk.shape[1]
    count = sum(r.shape[0] for r in rows)
    chunk = 1024
    down_ = lambda a: pl.BlockSpec((chunk, a.shape[1]), lambda i, s: (i, 0))
    whole = lambda a: pl.BlockSpec(a.shape, lambda i, s: (0, 0))
    wide = nq + 2 * nk + down.shape[1]
    return pl.pallas_call(
        functools.partial(project_kernel, bases=bases, parts=len(rows)),
        out_shape=(
            jax.ShapeDtypeStruct((count, nq), jnp.bfloat16),
            jax.ShapeDtypeStruct((count, 2 * nk), jnp.bfloat16),
        ),
        grid_spec=pltpu.PrefetchScalarGridSpec(
            num_scalar_prefetch=1,
            grid=(depth // chunk,),
            in_specs=[HELD] * len(rows)
            + [down_(w) for w in (wq, wk, wv, down)]
            + [whole(u) for u in (q_up, k_up, v_up)],
            out_specs=(HELD, HELD),
            scratch_shapes=[pltpu.VMEM((count, wide), jnp.float32)],
        ),
        compiler_params=pltpu.CompilerParams(vmem_limit_bytes=48 * MIB),
        cost_estimate=pl.CostEstimate(
            flops=2 * count * depth * wide,
            bytes_accessed=2 * depth * (wide + count),
            transcendentals=0,
        ),
    )(info, *rows, wq, wk, wv, down, q_up, k_up, v_up)


def positions(info, bases):
    tokens = len(bases) * PIECE
    column = lax.broadcasted_iota(jnp.int32, (1, GROUP * tokens), 1)
    pos = column
    for h in range(GROUP):
        for i, base in enumerate(bases):
            at = h * tokens + i * PIECE
            pos = jnp.where(column >= at, column + (info[base] - at), pos)
    return pos


def attend_kernel(info, q1, q2, *refs, sections, parts):
    shares, (out, kv, qt, acc, peak, held, held_peak) = refs[: len(parts)], refs[len(parts) :]
    for ref, (dx, dz, dc, at) in zip(shares, parts):
        x = lax.rem(info[23] + dx, 4)
        z = info[24] if dz == 0 else 1 - info[24]
        c = info[25] if dc == 0 else 1 - info[25]
        kv[x * 4 + z * 2 + c, at : at + ref.shape[0]] = ref[...]
    index = lax.broadcasted_iota(jnp.int32, (BLOCK, 1), 0)
    offsets = index
    for i, piece in enumerate(CHUNKS):
        offsets = jnp.where(index >= i * PIECE, index + (info[15 + piece] - i) * PIECE, offsets)

    def of_block(t, at):
        def spans():
            i = 0
            while i < len(CHUNKS):
                n = 1
                while i + n < len(CHUNKS) and (CHUNKS[i + n] < 4) == (CHUNKS[i] < 4):
                    n += 1
                device = t if CHUNKS[i] < 4 else t ^ OTHER
                yield kv[device, i * PIECE : (i + n) * PIECE, at : at + HEAD_SIZE]
                i += n

        return jnp.concatenate(list(spans()), axis=0)

    done = 0
    for pieces in sections:
        tokens = len(pieces) * PIECE
        total = GROUP * tokens
        width = WIDTH if total % WIDTH == 0 else PIECE * GROUP
        rows = []
        for piece in pieces:
            place = CHUNKS.index(piece)
            ref, place = (q1, place) if place < 4 else (q2, place - 4)
            rows.append(ref[place * PIECE : (place + 1) * PIECE])
        q = jnp.concatenate(rows, axis=0)
        q = [q[:, h * HEAD_SIZE : (h + 1) * HEAD_SIZE] for h in range(GROUP)]
        qt[:, :total] = jnp.concatenate(q, axis=0).T
        acc[:, :total] = jnp.zeros((HEAD_SIZE + 8, total), jnp.float32)
        peak[:, :total] = jnp.full((1, total), LEAST, jnp.float32)
        pos = positions(info, pieces)
        low = start_of(info, pos)
        first = last = info[pieces[0]]
        for piece in pieces[1:]:
            first, last = jnp.minimum(first, info[piece]), jnp.maximum(last, info[piece])
        last = last + (PIECE - 1)
        n0 = start_of(info, first) // BLOCK
        n3 = last // BLOCK + 1
        m1 = jnp.clip((start_of(info, last) + BLOCK - 1) // BLOCK, n0, n3)
        m2 = jnp.clip(first // BLOCK, m1, n3)
        ahead = m1 - n0

        def step(now, later, masked):
            if later is not None:
                keys = of_block(later, 0)
            if now is not None:
                values = jnp.concatenate(
                    [of_block(now, HEAD_SIZE).T, jnp.ones((8, BLOCK), jnp.bfloat16)], axis=0
                )
            for c in range(0, total, width):
                at = slice(c, c + width)
                if now is not None:
                    old = peak[:, at]
                    fresh = jnp.maximum(old, held_peak[:, at])
                    weights = jnp.exp2((held[:, at] - fresh) * EXP2_SCALE).astype(jnp.bfloat16)
                    decay = jnp.exp2((old - fresh) * EXP2_SCALE)
                    peak[:, at] = fresh
                if later is not None:
                    scores = jnp.dot(keys, qt[:, at], preferred_element_type=jnp.float32)
                    if masked:
                        key_pos = offsets + later * BLOCK
                        allowed = (key_pos <= pos[:, at]) & (key_pos >= low[:, at])
                        scores = jnp.where(allowed, scores, MASKED)
                    held[:, at] = scores
                    held_peak[:, at] = jnp.max(scores, axis=0, keepdims=True)
                if now is not None:
                    acc[:, at] = acc[:, at] * decay + jnp.dot(
                        values, weights, preferred_element_type=jnp.float32
                    )

        def masked_tile(i):
            return jnp.where(i < ahead, n0 + i, m2 + i - ahead)

        def masked_step(i, now):
            step(now, masked_tile(i), True)
            return masked_tile(i)

        def plain_step(j, now):
            step(now, j, False)
            return j

        step(None, masked_tile(0), True)
        now = lax.fori_loop(1, ahead + n3 - m2, masked_step, masked_tile(0))
        now = lax.fori_loop(m1, m2, plain_step, now)
        step(now, None, False)
        mixed = acc[:HEAD_SIZE, :total] / acc[HEAD_SIZE : HEAD_SIZE + 1, :total]
        mixed = mixed.T.astype(jnp.bfloat16)
        for h in range(GROUP):
            out[done : done + tokens, h * HEAD_SIZE : (h + 1) * HEAD_SIZE] = mixed[
                h * tokens : (h + 1) * tokens
            ]
        done += tokens


def attend(info, q1, q2, shares, sections):
    parts = [k[:4] for k in shares]
    arrays = [k[4] for k in shares]
    tokens = [len(s) * PIECE for s in sections]
    total = GROUP * max(tokens)
    out_shape = jax.ShapeDtypeStruct((sum(tokens), GROUP * HEAD_SIZE), jnp.bfloat16)
    return pl.pallas_call(
        functools.partial(attend_kernel, sections=sections, parts=parts),
        out_shape=out_shape,
        grid_spec=pltpu.PrefetchScalarGridSpec(
            num_scalar_prefetch=1,
            grid=(1,),
            in_specs=[HELD] * (2 + len(arrays)),
            out_specs=HELD,
            scratch_shapes=[
                pltpu.VMEM((BLOCKS, BLOCK, 2 * HEAD_SIZE), jnp.bfloat16),
                pltpu.VMEM((HEAD_SIZE, total), jnp.bfloat16),
                pltpu.VMEM((HEAD_SIZE + 8, total), jnp.float32),
                pltpu.VMEM((1, total), jnp.float32),
                pltpu.VMEM((BLOCK, total), jnp.float32),
                pltpu.VMEM((1, total), jnp.float32),
            ],
        ),
        compiler_params=pltpu.CompilerParams(vmem_limit_bytes=48 * MIB),
        cost_estimate=pl.CostEstimate(
            flops=4 * GROUP * sum(tokens) * BLOCKS * BLOCK * HEAD_SIZE,
            bytes_accessed=8 * MIB,
            transcendentals=GROUP * sum(tokens) * BLOCKS * BLOCK,
        ),
    )(info, q1, q2, *arrays)


def output_kernel(info, mixed, weight, down, up, *rest, bases):
    *outs, rows = rest
    depth = mixed.shape[1]

    @pl.when(pl.program_id(0) == 0)
    def _():
        lows = jnp.dot(mixed[...], down[...], preferred_element_type=jnp.float32)
        lows = jnp.where(keep_columns(info, bases, lows.shape[1]), ADAPTER_SCALE * lows, 0.0)
        rows[:, :depth] = mixed[...]
        rows[:, depth:] = lows.astype(jnp.bfloat16)

    weights = jnp.concatenate([weight[...], up[...]], axis=0)
    result = jnp.dot(rows[...], weights, preferred_element_type=jnp.float32).astype(jnp.bfloat16)
    chunk = weight.shape[1]
    columns = pl.ds(pl.multiple_of(pl.program_id(0) * chunk, chunk), chunk)
    for i, out in enumerate(outs):
        out[:, columns] = result[i * PIECE : (i + 1) * PIECE]


def output(info, mixed, weight, down, up, bases):
    features = weight.shape[1]
    chunk = 1024
    depth = weight.shape[0] + up.shape[0]
    whole = lambda a: pl.BlockSpec(a.shape, lambda i, s: (0, 0))
    across = lambda n: pl.BlockSpec((n, chunk), lambda i, s: (0, i))
    return pl.pallas_call(
        functools.partial(output_kernel, bases=bases),
        out_shape=(jax.ShapeDtypeStruct((PIECE, features), jnp.bfloat16),) * len(bases),
        grid_spec=pltpu.PrefetchScalarGridSpec(
            num_scalar_prefetch=1,
            grid=(features // chunk,),
            in_specs=[HELD, across(weight.shape[0]), whole(down), across(up.shape[0])],
            out_specs=(HELD,) * len(bases),
            scratch_shapes=[pltpu.VMEM((mixed.shape[0], depth), jnp.bfloat16)],
        ),
        compiler_params=pltpu.CompilerParams(vmem_limit_bytes=48 * MIB),
        cost_estimate=pl.CostEstimate(
            flops=2 * mixed.shape[0] * depth * features,
            bytes_accessed=2 * features * (depth + mixed.shape[0]),
            transcendentals=0,
        ),
    )(info, mixed, weight, down, up)


def normalize(activations, input_norm_gain):
    values = activations.astype(jnp.float32)
    power = jnp.mean(values * values, axis=1, keepdims=True)
    return (values * lax.rsqrt(power + EPS_NORM) * input_norm_gain[None, :]).astype(jnp.bfloat16)


def along_y(rows, hop):
    return lax.ppermute(
        rows, "uly", [(z * 4 + y, z * 4 + (y + hop) % 4) for z in range(2) for y in range(4)]
    )


def across_z(rows):
    pairs = [(b * 8 + u, (b ^ OTHER) * 8 + (u ^ 4)) for b in range(16) for u in range(8)]
    return lax.ppermute(rows, ("blk", "uly"), pairs)


def flipped(rows, bit):
    return lax.ppermute(rows, "blk", [(b, b ^ bit) for b in range(16)])


def along_x(rows, hop):
    return lax.ppermute(rows, "blk", [(b, (b + 4 * hop) % 16) for b in range(16)])


def at_once(kv):
    found = [(0, 0, 0, kv)]
    for hop in (2, 1, 3):
        for dz in (1, 0):
            pairs = [(b, ((b + 4 * hop) % 16) ^ (2 * dz)) for b in range(16)]
            found.append((4 - hop, dz, 0, lax.ppermute(kv, "blk", pairs)))
    return found + [(0, 1, 0, flipped(kv, 2))]


def in_steps(kv, at):
    mid = HALF // 2
    other, from_m, from_p = flipped(kv, 2), along_x(kv, 1), along_x(kv, -1)
    top, end = along_x(from_m[:mid], 1), along_x(from_p[mid:], -1)
    other_m, other_p = along_x(other, 1), along_x(other, -1)
    other_far = flipped(jnp.concatenate([top, end], axis=0), 2)
    return [
        (0, 0, at, kv),
        (3, 0, at, from_m),
        (1, 0, at, from_p),
        (0, 1, at, other),
        (2, 0, at, top),
        (2, 0, at + mid, end),
        (3, 1, at, other_m),
        (1, 1, at, other_p),
        (2, 1, at, other_far),
    ]


def both_cores(found):
    return [(dx, dz, 0, at, a) for dx, dz, at, a in found] + [
        (dx, dz, 1, at, flipped(a, 1)) for dx, dz, at, a in found
    ]


def plan(segment_index, segment_adapter):
    block, head = lax.axis_index("blk"), lax.axis_index("uly")
    z, y = head // 4, head % 4
    ys = [y, (y + 3) % 4, (y + 1) % 4, (y + 2) % 4]
    here = [z * 4 + p for p in ys]
    there = [(1 - z) * 4 + p for p in ys]
    firsts = [block * BLOCK + p * PIECE for p in here]
    firsts += [(block ^ OTHER) * BLOCK + p * PIECE for p in there]
    ends = jnp.sum(
        segment_index[None, :] < jnp.arange(1, 4, dtype=jnp.int32)[:, None], axis=1, dtype=jnp.int32
    )
    return jnp.concatenate(
        [
            jnp.stack(firsts).astype(jnp.int32),
            ends,
            segment_adapter,
            jnp.stack(here + there).astype(jnp.int32),
            jnp.stack([block // 4, (block // 2) % 2, block % 2]).astype(jnp.int32),
        ]
    )


def added(*terms):
    return sum(t.astype(jnp.float32) for t in terms).astype(jnp.bfloat16)


def shards(
    activations,
    input_norm_gain,
    query_weight,
    key_weight,
    value_weight,
    output_weight,
    adapter_down_maps,
    query_up_maps,
    key_up_maps,
    value_up_maps,
    output_down_maps,
    output_up_maps,
    segment_index,
    segment_adapter,
):
    info = plan(segment_index, segment_adapter)
    weights = (
        query_weight,
        key_weight,
        value_weight,
        adapter_down_maps,
        query_up_maps,
        key_up_maps,
        value_up_maps,
    )
    mid = PIECE // 2
    own = normalize(activations, input_norm_gain)
    own_m, own_p, other = along_y(own, 1), along_y(own, -1), across_z(own)
    far_top, far_end = along_y(own_m[:mid], 1), along_y(own_p[mid:], -1)
    other_m, other_p = along_y(other, 1), along_y(other, -1)
    other_far = across_z(jnp.concatenate([far_top, far_end], axis=0))

    q1, kv1 = project(info, [own, own_m, own_p, other], CHUNKS[:4], *weights)
    found1 = at_once(kv1)
    q2, kv2 = project(info, [far_top, far_end, other_m, other_p, other_far], CHUNKS[4:], *weights)
    kv2, *arrays = lax.optimization_barrier((kv2, *[f[3] for f in found1]))
    found1 = [(*f[:3], a) for f, a in zip(found1, arrays)]
    shares = both_cores(in_steps(kv2, HALF)) + both_cores(found1)

    out_weights = (output_weight, output_down_maps, output_up_maps)
    mixed = attend(info, q1, q2, shares, ((4, 5, 6, 7),))
    b0, bm, bp, bf = output(info, mixed, *out_weights, (4, 5, 6, 7))
    for_far = across_z(bf)
    for_other = added(b0, along_y(bp, 1), along_y(bm, -1))
    mixed = attend(info, q1, q2, shares, ((0, 1, 2, 3),))
    a0, am, ap, af = output(info, mixed, *out_weights, (0, 1, 2, 3))
    far = added(af, for_far)
    top, end = along_y(far[:mid], 1), along_y(far[mid:], -1)
    to_p = added(ap, jnp.pad(top, ((0, mid), (0, 0))))
    to_m = added(am, jnp.pad(end, ((mid, 0), (0, 0))))
    return added(a0, along_y(to_p, 1), along_y(to_m, -1), across_z(for_other))


def solution(mesh):
    return jax.shard_map(
        shards,
        mesh=mesh,
        in_specs=(
            P(("blk", "uly"), None),
            P(),
            P(None, "uly"),
            P(None, "uly"),
            P(None, "uly"),
            P("uly", None),
            P(),
            P(None, "uly"),
            P(None, "uly"),
            P(None, "uly"),
            P("uly", None),
            P(),
            P(),
            P(),
        ),
        out_specs=P(("blk", "uly"), None),
        check_vma=False,
    )
```

```python
import functools
import math

import jax
import jax.numpy as jnp
from jax import lax
from jax.experimental import pallas as pl
from jax.experimental.pallas import tpu as pltpu
from jax.sharding import PartitionSpec as P

HEAD_SIZE = 128
ADAPTER_RANK = 16
ADAPTER_COUNT = 8
GROUP = 4
PIECE = 96
HALF = 384
BLOCK = 768
BLOCKS = 16
OTHER = 2
EPS_NORM = 1e-05
ADAPTER_SCALE = 2.0
MASKED = -1e30
LEAST = -1e20
EXP2_SCALE = math.log2(math.e) / math.sqrt(HEAD_SIZE)
MIB = 2**20
HELD = pl.BlockSpec(memory_space=pltpu.VMEM)
CHUNKS = (0, 1, 2, 4, 3, 5, 6, 7)
WIDTH = 512

INFO = 26


def pos_of(info, bases, width, axis):
    shape = (width * len(bases), 1) if axis == 0 else (1, width * len(bases))
    index = lax.broadcasted_iota(jnp.int32, shape, axis)
    pos = index + info[bases[0]]
    for i, base in enumerate(bases[1:], 1):
        pos = jnp.where(index >= i * width, index + (info[base] - i * width), pos)
    return pos


def start_of(info, pos):
    start = jnp.zeros_like(pos)
    for s in range(8, 11):
        start = jnp.where(pos >= info[s], info[s], start)
    return start


def tenant_of(info, pos):
    tenant = jnp.zeros_like(pos) + info[11]
    for s in range(3):
        tenant = jnp.where(pos >= info[8 + s], info[12 + s], tenant)
    return tenant


def keep_columns(info, bases, columns):
    tenant = tenant_of(info, pos_of(info, bases, PIECE, 0))
    column = lax.broadcasted_iota(jnp.int32, (len(bases) * PIECE, columns), 1)
    return (column // ADAPTER_RANK) % ADAPTER_COUNT == tenant


def project_kernel(info, *refs, bases, parts, targets, earlier):
    rows, refs = refs[:parts], refs[parts:]
    if earlier:
        before, refs = refs[0], refs[1:]
    down, weights, ups = refs[0], refs[1 : 1 + len(targets)], refs[1 + len(targets) : -2]
    out, acc = refs[-2:]
    step = pl.program_id(0)
    hidden = ADAPTER_COUNT * ADAPTER_RANK
    chunk = down.shape[0] // pl.num_programs(0)
    columns = pl.ds(pl.multiple_of(step * chunk, chunk), chunk)
    x = jnp.concatenate([r[:, columns] for r in rows], axis=0)
    w = [w[columns] for w in weights]
    w += [down[columns, t * hidden : (t + 1) * hidden] for t in targets]
    product = jnp.dot(x, jnp.concatenate(w, axis=1), preferred_element_type=jnp.float32)

    @pl.when(step == 0)
    def _():
        acc[...] = product

    @pl.when(step > 0)
    def _():
        acc[...] += product

    @pl.when(step == pl.num_programs(0) - 1)
    def _():
        keep = keep_columns(info, bases, hidden)
        new = 0
        if earlier:
            new = before.shape[0]
            out[:new] = before[...]
        at, low_at = 0, out.shape[1]
        for weight, up in zip(weights, ups):
            width = weight.shape[1]
            low = jnp.where(keep, acc[:, low_at : low_at + hidden], 0.0).astype(jnp.bfloat16)
            adapted = jnp.dot(low, up[...], preferred_element_type=jnp.float32)
            out[new:, at : at + width] = (
                acc[:, at : at + width] + ADAPTER_SCALE * adapted
            ).astype(jnp.bfloat16)
            at += width
            low_at += hidden


def project(info, rows, bases, down, targets, weights, ups, before=()):
    depth, count = down.shape[0], sum(r.shape[0] for r in rows)
    width = sum(w.shape[1] for w in weights)
    wide = width + ADAPTER_COUNT * ADAPTER_RANK * len(targets)
    return pl.pallas_call(
        functools.partial(
            project_kernel,
            bases=bases,
            parts=len(rows),
            targets=targets,
            earlier=bool(before),
        ),
        out_shape=jax.ShapeDtypeStruct((count + sum(b.shape[0] for b in before), width), jnp.bfloat16),
        grid_spec=pltpu.PrefetchScalarGridSpec(
            num_scalar_prefetch=1,
            grid=(depth // 1024,),
            in_specs=[HELD] * (len(rows) + len(before) + 1 + 2 * len(targets)),
            out_specs=HELD,
            scratch_shapes=[pltpu.VMEM((count, wide), jnp.float32)],
        ),
        compiler_params=pltpu.CompilerParams(vmem_limit_bytes=14 * MIB),
        cost_estimate=pl.CostEstimate(
            flops=4 * count * depth * wide,
            bytes_accessed=2 * depth * (wide + count),
            transcendentals=0,
        ),
    )(info, *rows, *before, down, *weights, *ups)


def positions(info, bases):
    tokens = len(bases) * PIECE
    column = lax.broadcasted_iota(jnp.int32, (1, GROUP * tokens), 1)
    pos = column
    for h in range(GROUP):
        for i, base in enumerate(bases):
            at = h * tokens + i * PIECE
            pos = jnp.where(column >= at, column + (info[base] - at), pos)
    return pos


def attend_kernel(info, q1, q2, *refs, sections, parts):
    shares, (out, kv, qt, acc, peak, held, held_peak) = refs[: len(parts)], refs[len(parts) :]
    for ref, (dx, dz, dc, at) in zip(shares, parts):
        x = lax.rem(info[23] + dx, 4)
        z = info[24] if dz == 0 else 1 - info[24]
        c = info[25] if dc == 0 else 1 - info[25]
        kv[x * 4 + z * 2 + c, at : at + ref.shape[0]] = ref[...]
    index = lax.broadcasted_iota(jnp.int32, (BLOCK, 1), 0)
    offsets = index
    for i, piece in enumerate(CHUNKS):
        offsets = jnp.where(index >= i * PIECE, index + (info[15 + piece] - i) * PIECE, offsets)

    def of_block(t, at):
        def spans():
            i = 0
            while i < len(CHUNKS):
                n = 1
                while i + n < len(CHUNKS) and (CHUNKS[i + n] < 4) == (CHUNKS[i] < 4):
                    n += 1
                device = t if CHUNKS[i] < 4 else t ^ OTHER
                yield kv[device, i * PIECE : (i + n) * PIECE, at : at + HEAD_SIZE]
                i += n

        return jnp.concatenate(list(spans()), axis=0)

    done = 0
    for pieces in sections:
        tokens = len(pieces) * PIECE
        total = GROUP * tokens
        width = WIDTH if total % WIDTH == 0 else PIECE * GROUP
        rows = []
        for piece in pieces:
            place = CHUNKS.index(piece)
            ref, place = (q1, place) if place < 4 else (q2, place - 4)
            rows.append(ref[place * PIECE : (place + 1) * PIECE])
        q = jnp.concatenate(rows, axis=0)
        q = [q[:, h * HEAD_SIZE : (h + 1) * HEAD_SIZE] for h in range(GROUP)]
        qt[:, :total] = jnp.concatenate(q, axis=0).T
        acc[:, :total] = jnp.zeros((HEAD_SIZE + 8, total), jnp.float32)
        peak[:, :total] = jnp.full((1, total), LEAST, jnp.float32)
        pos = positions(info, pieces)
        low = start_of(info, pos)
        first = last = info[pieces[0]]
        for piece in pieces[1:]:
            first, last = jnp.minimum(first, info[piece]), jnp.maximum(last, info[piece])
        last = last + (PIECE - 1)
        n0 = start_of(info, first) // BLOCK
        n3 = last // BLOCK + 1
        m1 = jnp.clip((start_of(info, last) + BLOCK - 1) // BLOCK, n0, n3)
        m2 = jnp.clip(first // BLOCK, m1, n3)
        ahead = m1 - n0

        def step(now, later, masked):
            if later is not None:
                keys = of_block(later, 0)
            if now is not None:
                values = jnp.concatenate(
                    [of_block(now, HEAD_SIZE).T, jnp.ones((8, BLOCK), jnp.bfloat16)], axis=0
                )
            for c in range(0, total, width):
                at = slice(c, c + width)
                if now is not None:
                    old = peak[:, at]
                    fresh = jnp.maximum(old, held_peak[:, at])
                    weights = jnp.exp2((held[:, at] - fresh) * EXP2_SCALE).astype(jnp.bfloat16)
                    decay = jnp.exp2((old - fresh) * EXP2_SCALE)
                    peak[:, at] = fresh
                if later is not None:
                    scores = jnp.dot(keys, qt[:, at], preferred_element_type=jnp.float32)
                    if masked:
                        key_pos = offsets + later * BLOCK
                        allowed = (key_pos <= pos[:, at]) & (key_pos >= low[:, at])
                        scores = jnp.where(allowed, scores, MASKED)
                    held[:, at] = scores
                    held_peak[:, at] = jnp.max(scores, axis=0, keepdims=True)
                if now is not None:
                    acc[:, at] = acc[:, at] * decay + jnp.dot(
                        values, weights, preferred_element_type=jnp.float32
                    )

        def masked_tile(i):
            return jnp.where(i < ahead, n0 + i, m2 + i - ahead)

        def masked_step(i, now):
            step(now, masked_tile(i), True)
            return masked_tile(i)

        def plain_step(j, now):
            step(now, j, False)
            return j

        step(None, masked_tile(0), True)
        now = lax.fori_loop(1, ahead + n3 - m2, masked_step, masked_tile(0))
        now = lax.fori_loop(m1, m2, plain_step, now)
        step(now, None, False)
        mixed = acc[:HEAD_SIZE, :total] / acc[HEAD_SIZE : HEAD_SIZE + 1, :total]
        mixed = mixed.T.astype(jnp.bfloat16)
        for h in range(GROUP):
            out[done : done + tokens, h * HEAD_SIZE : (h + 1) * HEAD_SIZE] = mixed[
                h * tokens : (h + 1) * tokens
            ]
        done += tokens


def attend(info, queries, shares, sections):
    parts = [k[:4] for k in shares]
    arrays = [k[4] for k in shares]
    tokens = [len(s) * PIECE for s in sections]
    total = GROUP * max(tokens)
    out_shape = jax.ShapeDtypeStruct((sum(tokens), GROUP * HEAD_SIZE), jnp.bfloat16)
    return pl.pallas_call(
        functools.partial(attend_kernel, sections=sections, parts=parts),
        out_shape=out_shape,
        grid_spec=pltpu.PrefetchScalarGridSpec(
            num_scalar_prefetch=1,
            grid=(1,),
            in_specs=[HELD] * (2 + len(arrays)),
            out_specs=pl.BlockSpec(out_shape.shape, lambda i, s: (0, 0)),
            scratch_shapes=[
                pltpu.VMEM((BLOCKS, BLOCK, 2 * HEAD_SIZE), jnp.bfloat16),
                pltpu.VMEM((HEAD_SIZE, total), jnp.bfloat16),
                pltpu.VMEM((HEAD_SIZE + 8, total), jnp.float32),
                pltpu.VMEM((1, total), jnp.float32),
                pltpu.VMEM((BLOCK, total), jnp.float32),
                pltpu.VMEM((1, total), jnp.float32),
            ],
        ),
        compiler_params=pltpu.CompilerParams(vmem_limit_bytes=24 * MIB),
        cost_estimate=pl.CostEstimate(
            flops=4 * GROUP * sum(tokens) * BLOCKS * BLOCK * HEAD_SIZE,
            bytes_accessed=8 * MIB,
            transcendentals=GROUP * sum(tokens) * BLOCKS * BLOCK,
        ),
    )(info, *queries, *arrays)


def output_kernel(info, mixed, weight, down, up, *rest, bases):
    *outs, rows = rest
    depth = mixed.shape[1]

    @pl.when(pl.program_id(0) == 0)
    def _():
        lows = jnp.dot(mixed[...], down[...], preferred_element_type=jnp.float32)
        lows = jnp.where(keep_columns(info, bases, lows.shape[1]), ADAPTER_SCALE * lows, 0.0)
        rows[:, :depth] = mixed[...]
        rows[:, depth:] = lows.astype(jnp.bfloat16)

    chunk = up.shape[1] // pl.num_programs(0)
    columns = pl.ds(pl.multiple_of(pl.program_id(0) * chunk, chunk), chunk)
    weights = jnp.concatenate([weight[:, columns], up[:, columns]], axis=0)
    result = jnp.dot(rows[...], weights, preferred_element_type=jnp.float32).astype(jnp.bfloat16)
    for i, out in enumerate(outs):
        out[:, columns] = result[i * PIECE : (i + 1) * PIECE]


def output(info, mixed, weight, down, up, bases):
    features = weight.shape[1]
    chunk = 1024
    depth = weight.shape[0] + up.shape[0]
    return pl.pallas_call(
        functools.partial(output_kernel, bases=bases),
        out_shape=(jax.ShapeDtypeStruct((PIECE, features), jnp.bfloat16),) * len(bases),
        grid_spec=pltpu.PrefetchScalarGridSpec(
            num_scalar_prefetch=1,
            grid=(features // chunk,),
            in_specs=[HELD] * 4,
            out_specs=(HELD,) * len(bases),
            scratch_shapes=[pltpu.VMEM((mixed.shape[0], depth), jnp.bfloat16)],
        ),
        compiler_params=pltpu.CompilerParams(vmem_limit_bytes=12 * MIB),
        cost_estimate=pl.CostEstimate(
            flops=2 * mixed.shape[0] * depth * features,
            bytes_accessed=2 * features * (depth + mixed.shape[0]),
            transcendentals=0,
        ),
    )(info, mixed, weight, down, up)


def normalize_kernel(activations, gain, out):
    values = activations[...].astype(jnp.float32)
    power = jnp.mean(values * values, axis=1, keepdims=True)
    out[...] = (values * lax.rsqrt(power + EPS_NORM) * gain[...]).astype(jnp.bfloat16)


def normalize(activations, input_norm_gain):
    rows, features = activations.shape
    step = 32
    return pl.pallas_call(
        normalize_kernel,
        out_shape=jax.ShapeDtypeStruct(activations.shape, jnp.bfloat16),
        grid=(rows // step,),
        in_specs=[
            pl.BlockSpec((step, features), lambda i: (i, 0)),
            pl.BlockSpec((1, features), lambda i: (0, 0)),
        ],
        out_specs=pl.BlockSpec((step, features), lambda i: (i, 0)),
        compiler_params=pltpu.CompilerParams(vmem_limit_bytes=12 * MIB),
    )(activations, input_norm_gain[None, :])


def along_y(rows, hop):
    return lax.ppermute(
        rows, "uly", [(z * 4 + y, z * 4 + (y + hop) % 4) for z in range(2) for y in range(4)]
    )


def across_z(rows):
    pairs = [(b * 8 + u, (b ^ OTHER) * 8 + (u ^ 4)) for b in range(16) for u in range(8)]
    return lax.ppermute(rows, ("blk", "uly"), pairs)


def flipped(rows, bit):
    return lax.ppermute(rows, "blk", [(b, b ^ bit) for b in range(16)])


def along_x(rows, hop):
    return lax.ppermute(rows, "blk", [(b, (b + 4 * hop) % 16) for b in range(16)])


def in_steps(kv, other, from_m, from_p):
    mid = BLOCK // 2
    top, end = along_x(from_m[:mid], 1), along_x(from_p[mid:], -1)
    other_m, other_p = along_x(other, 1), along_x(other, -1)
    other_far = flipped(jnp.concatenate([top, end], axis=0), 2)
    return [
        (0, 0, 0, kv),
        (3, 0, 0, from_m),
        (1, 0, 0, from_p),
        (0, 1, 0, other),
        (2, 0, 0, top),
        (2, 0, mid, end),
        (3, 1, 0, other_m),
        (1, 1, 0, other_p),
        (2, 1, 0, other_far),
    ]


def both_cores(found):
    return [(dx, dz, 0, at, a) for dx, dz, at, a in found] + [
        (dx, dz, 1, at, flipped(a, 1)) for dx, dz, at, a in found
    ]


def plan(segment_index, segment_adapter):
    block, head = lax.axis_index("blk"), lax.axis_index("uly")
    z, y = head // 4, head % 4
    ys = [y, (y + 3) % 4, (y + 1) % 4, (y + 2) % 4]
    here = [z * 4 + p for p in ys]
    there = [(1 - z) * 4 + p for p in ys]
    firsts = [block * BLOCK + p * PIECE for p in here]
    firsts += [(block ^ OTHER) * BLOCK + p * PIECE for p in there]
    ends = jnp.sum(
        segment_index[None, :] < jnp.arange(1, 4, dtype=jnp.int32)[:, None], axis=1, dtype=jnp.int32
    )
    return jnp.concatenate(
        [
            jnp.stack(firsts).astype(jnp.int32),
            ends,
            segment_adapter,
            jnp.stack(here + there).astype(jnp.int32),
            jnp.stack([block // 4, (block // 2) % 2, block % 2]).astype(jnp.int32),
        ]
    )


def added(*terms):
    return sum(t.astype(jnp.float32) for t in terms).astype(jnp.bfloat16)


def shards(
    activations,
    input_norm_gain,
    query_weight,
    key_weight,
    value_weight,
    output_weight,
    adapter_down_maps,
    query_up_maps,
    key_up_maps,
    value_up_maps,
    output_down_maps,
    output_up_maps,
    segment_index,
    segment_adapter,
):
    info = plan(segment_index, segment_adapter)
    mid = PIECE // 2
    own = normalize(activations, input_norm_gain)
    own_m, own_p, other = along_y(own, 1), along_y(own, -1), across_z(own)
    far_top, far_end = along_y(own_m[:mid], 1), along_y(own_p[mid:], -1)
    other_m, other_p = along_y(other, 1), along_y(other, -1)
    other_far = across_z(jnp.concatenate([far_top, far_end], axis=0))

    down = adapter_down_maps
    kv_weights, kv_ups = (key_weight, value_weight), (key_up_maps, value_up_maps)
    rows1 = [own, own_m, own_p, other]
    rows2 = [far_top, far_end, other_m, other_p, other_far]
    kv = project(info, rows1, CHUNKS[:4], down, (1, 2), kv_weights, kv_ups)
    q_operands = (down, (0,), (query_weight,), (query_up_maps,))
    q1 = project(info, rows1, CHUNKS[:4], *q_operands)
    kv, q1 = lax.optimization_barrier((kv, q1))
    kv = project(info, rows2, CHUNKS[4:], down, (1, 2), kv_weights, kv_ups, before=(kv,))
    other, from_m, from_p = flipped(kv, 2), along_x(kv, 1), along_x(kv, -1)
    q2 = project(info, rows2, CHUNKS[4:], *q_operands)
    other, from_m, from_p, q2 = lax.optimization_barrier((other, from_m, from_p, q2))
    shares = both_cores(in_steps(kv, other, from_m, from_p))
    queries = (q1, q2)

    def products(queries, *sections):
        mixed = attend(info, queries, shares, sections)
        order = sum(sections, ())
        return output(info, mixed, output_weight, output_down_maps, output_up_maps, order)

    bf, bm, bp = products(queries, (7, 5, 6))
    for_far, from_m, from_p = across_z(bf), along_y(bp, 1), along_y(bm, -1)
    af, am, ap, b0 = products(queries, (3, 1, 2), (4,))
    far = added(af, for_far)
    other_sum = added(b0, from_m, from_p)
    queries, far, other_sum = lax.optimization_barrier((queries, far, other_sum))
    top, end = along_y(far[:mid], 1), along_y(far[mid:], -1)
    for_own = across_z(other_sum)
    (a0,) = products(queries, (0,))
    to_p = added(ap, jnp.pad(top, ((0, mid), (0, 0))))
    to_m = added(am, jnp.pad(end, ((mid, 0), (0, 0))))
    return added(a0, along_y(to_p, 1), along_y(to_m, -1), for_own)


def solution(mesh):
    return jax.shard_map(
        shards,
        mesh=mesh,
        in_specs=(
            P(("blk", "uly"), None),
            P(),
            P(None, "uly"),
            P(None, "uly"),
            P(None, "uly"),
            P("uly", None),
            P(),
            P(None, "uly"),
            P(None, "uly"),
            P(None, "uly"),
            P("uly", None),
            P(),
            P(),
            P(),
        ),
        out_specs=P(("blk", "uly"), None),
        check_vma=False,
    )
```

```python
import functools
import math

import jax
import jax.numpy as jnp
from jax import lax
from jax.experimental import pallas as pl
from jax.experimental.pallas import tpu as pltpu
from jax.sharding import PartitionSpec as P

HEAD_SIZE = 128
ADAPTER_RANK = 16
ADAPTER_COUNT = 8
GROUP = 4
PIECE = 96
HALF = 384
BLOCK = 768
BLOCKS = 16
OTHER = 2
EPS_NORM = 1e-05
ADAPTER_SCALE = 2.0
MASKED = -1e30
LEAST = -1e20
EXP2_SCALE = math.log2(math.e) / math.sqrt(HEAD_SIZE)
MIB = 2**20
HELD = pl.BlockSpec(memory_space=pltpu.VMEM)
CHUNKS = (0, 1, 2, 4, 3, 5, 6, 7)
WIDTH = 512

INFO = 26


def pos_of(info, bases, width, axis):
    shape = (width * len(bases), 1) if axis == 0 else (1, width * len(bases))
    index = lax.broadcasted_iota(jnp.int32, shape, axis)
    pos = index + info[bases[0]]
    for i, base in enumerate(bases[1:], 1):
        pos = jnp.where(index >= i * width, index + (info[base] - i * width), pos)
    return pos


def start_of(info, pos):
    start = jnp.zeros_like(pos)
    for s in range(8, 11):
        start = jnp.where(pos >= info[s], info[s], start)
    return start


def tenant_of(info, pos):
    tenant = jnp.zeros_like(pos) + info[11]
    for s in range(3):
        tenant = jnp.where(pos >= info[8 + s], info[12 + s], tenant)
    return tenant


def keep_columns(info, bases, columns):
    tenant = tenant_of(info, pos_of(info, bases, PIECE, 0))
    column = lax.broadcasted_iota(jnp.int32, (len(bases) * PIECE, columns), 1)
    return (column // ADAPTER_RANK) % ADAPTER_COUNT == tenant


def project_kernel(info, *refs, bases, parts, targets, earlier):
    rows, refs = refs[:parts], refs[parts:]
    if earlier:
        before, refs = refs[0], refs[1:]
    down, weights, ups = refs[0], refs[1 : 1 + len(targets)], refs[1 + len(targets) : -2]
    out, acc = refs[-2:]
    step = pl.program_id(0)
    hidden = ADAPTER_COUNT * ADAPTER_RANK
    chunk = down.shape[0] // pl.num_programs(0)
    columns = pl.ds(pl.multiple_of(step * chunk, chunk), chunk)
    x = jnp.concatenate([r[:, columns] for r in rows], axis=0)
    w = [w[columns] for w in weights]
    w += [down[columns, t * hidden : (t + 1) * hidden] for t in targets]
    product = jnp.dot(x, jnp.concatenate(w, axis=1), preferred_element_type=jnp.float32)

    @pl.when(step == 0)
    def _():
        acc[...] = product

    @pl.when(step > 0)
    def _():
        acc[...] += product

    @pl.when(step == pl.num_programs(0) - 1)
    def _():
        keep = keep_columns(info, bases, hidden)
        new = 0
        if earlier:
            new = before.shape[0]
            out[:new] = before[...]
        at, low_at = 0, out.shape[1]
        for weight, up in zip(weights, ups):
            width = weight.shape[1]
            low = jnp.where(keep, acc[:, low_at : low_at + hidden], 0.0).astype(jnp.bfloat16)
            adapted = jnp.dot(low, up[...], preferred_element_type=jnp.float32)
            out[new:, at : at + width] = (
                acc[:, at : at + width] + ADAPTER_SCALE * adapted
            ).astype(jnp.bfloat16)
            at += width
            low_at += hidden


def project(info, rows, bases, down, targets, weights, ups, before=()):
    depth, count = down.shape[0], sum(r.shape[0] for r in rows)
    width = sum(w.shape[1] for w in weights)
    wide = width + ADAPTER_COUNT * ADAPTER_RANK * len(targets)
    return pl.pallas_call(
        functools.partial(
            project_kernel,
            bases=bases,
            parts=len(rows),
            targets=targets,
            earlier=bool(before),
        ),
        out_shape=jax.ShapeDtypeStruct((count + sum(b.shape[0] for b in before), width), jnp.bfloat16),
        grid_spec=pltpu.PrefetchScalarGridSpec(
            num_scalar_prefetch=1,
            grid=(depth // 1024,),
            in_specs=[HELD] * (len(rows) + len(before) + 1 + 2 * len(targets)),
            out_specs=HELD,
            scratch_shapes=[pltpu.VMEM((count, wide), jnp.float32)],
        ),
        compiler_params=pltpu.CompilerParams(vmem_limit_bytes=14 * MIB),
        cost_estimate=pl.CostEstimate(
            flops=4 * count * depth * wide,
            bytes_accessed=2 * depth * (wide + count),
            transcendentals=0,
        ),
    )(info, *rows, *before, down, *weights, *ups)


def positions(info, bases):
    tokens = len(bases) * PIECE
    column = lax.broadcasted_iota(jnp.int32, (1, GROUP * tokens), 1)
    pos = column
    for h in range(GROUP):
        for i, base in enumerate(bases):
            at = h * tokens + i * PIECE
            pos = jnp.where(column >= at, column + (info[base] - at), pos)
    return pos


def attend_kernel(info, q1, q2, *refs, sections, parts):
    shares, refs = refs[: len(parts)], refs[len(parts) :]
    if parts:
        out, kv, qt, acc, peak, held, held_peak = refs
    else:
        kv, out, qt, acc, peak, held, held_peak = refs
    for ref, (dx, dz, dc, at) in zip(shares, parts):
        x = lax.rem(info[23] + dx, 4)
        z = info[24] if dz == 0 else 1 - info[24]
        c = info[25] if dc == 0 else 1 - info[25]
        kv[x * 4 + z * 2 + c, at : at + ref.shape[0]] = ref[...]
    index = lax.broadcasted_iota(jnp.int32, (BLOCK, 1), 0)
    offsets = index
    for i, piece in enumerate(CHUNKS):
        offsets = jnp.where(index >= i * PIECE, index + (info[15 + piece] - i) * PIECE, offsets)

    def of_block(t, at):
        def spans():
            i = 0
            while i < len(CHUNKS):
                n = 1
                while i + n < len(CHUNKS) and (CHUNKS[i + n] < 4) == (CHUNKS[i] < 4):
                    n += 1
                device = t if CHUNKS[i] < 4 else t ^ OTHER
                yield kv[device, i * PIECE : (i + n) * PIECE, at : at + HEAD_SIZE]
                i += n

        return jnp.concatenate(list(spans()), axis=0)

    done = 0
    for pieces in sections:
        tokens = len(pieces) * PIECE
        total = GROUP * tokens
        width = WIDTH if total % WIDTH == 0 else PIECE * GROUP
        rows = []
        for piece in pieces:
            place = CHUNKS.index(piece)
            ref, place = (q1, place) if place < 4 else (q2, place - 4)
            rows.append(ref[place * PIECE : (place + 1) * PIECE])
        q = jnp.concatenate(rows, axis=0)
        q = [q[:, h * HEAD_SIZE : (h + 1) * HEAD_SIZE] for h in range(GROUP)]
        qt[:, :total] = jnp.concatenate(q, axis=0).T
        acc[:, :total] = jnp.zeros((HEAD_SIZE + 8, total), jnp.float32)
        peak[:, :total] = jnp.full((1, total), LEAST, jnp.float32)
        pos = positions(info, pieces)
        low = start_of(info, pos)
        first = last = info[pieces[0]]
        for piece in pieces[1:]:
            first, last = jnp.minimum(first, info[piece]), jnp.maximum(last, info[piece])
        last = last + (PIECE - 1)
        n0 = start_of(info, first) // BLOCK
        own = first // BLOCK
        m1 = jnp.clip((start_of(info, last) + BLOCK - 1) // BLOCK, n0, own)

        def step(now, later, causal=False, starts=False):
            if later is not None:
                keys = of_block(later, 0)
            if now is not None:
                values = jnp.concatenate(
                    [of_block(now, HEAD_SIZE).T, jnp.ones((8, BLOCK), jnp.bfloat16)], axis=0
                )
            for c in range(0, total, width):
                at = slice(c, c + width)
                if now is not None:
                    old = peak[:, at]
                    fresh = jnp.maximum(old, held_peak[:, at])
                    weights = jnp.exp2((held[:, at] - fresh) * EXP2_SCALE).astype(jnp.bfloat16)
                    decay = jnp.exp2((old - fresh) * EXP2_SCALE)
                    peak[:, at] = fresh
                if later is not None:
                    scores = jnp.dot(keys, qt[:, at], preferred_element_type=jnp.float32)
                    if causal or starts:
                        key_pos = offsets + later * BLOCK
                        allowed = key_pos >= low[:, at]
                        if causal:
                            allowed &= key_pos <= pos[:, at]
                        scores = jnp.where(allowed, scores, MASKED)
                    held[:, at] = scores
                    held_peak[:, at] = jnp.max(scores, axis=0, keepdims=True)
                if now is not None:
                    acc[:, at] = acc[:, at] * decay + jnp.dot(
                        values, weights, preferred_element_type=jnp.float32
                    )

        def starting_step(j, now):
            step(now, j, starts=True)
            return j

        def plain_step(j, now):
            step(now, j)
            return j

        step(None, own, causal=True)
        now = lax.fori_loop(n0, m1, starting_step, own)
        now = lax.fori_loop(m1, own, plain_step, now)
        step(now, None)
        mixed = acc[:HEAD_SIZE, :total] / acc[HEAD_SIZE : HEAD_SIZE + 1, :total]
        mixed = mixed.T.astype(jnp.bfloat16)
        for h in range(GROUP):
            out[done : done + tokens, h * HEAD_SIZE : (h + 1) * HEAD_SIZE] = mixed[
                h * tokens : (h + 1) * tokens
            ]
        done += tokens


def attend(info, queries, sections, shares=(), kv=None):
    parts = [k[:4] for k in shares]
    arrays = [k[4] for k in shares] if kv is None else [kv]
    tokens = [len(s) * PIECE for s in sections]
    total = GROUP * max(tokens)
    out_shape = jax.ShapeDtypeStruct((sum(tokens), GROUP * HEAD_SIZE), jnp.bfloat16)
    out_specs = pl.BlockSpec(out_shape.shape, lambda i, s: (0, 0))
    if kv is None:
        out_shape = (out_shape, jax.ShapeDtypeStruct((BLOCKS, BLOCK, 2 * HEAD_SIZE), jnp.bfloat16))
        out_specs = (out_specs, HELD)
    return pl.pallas_call(
        functools.partial(attend_kernel, sections=sections, parts=parts),
        out_shape=out_shape,
        grid_spec=pltpu.PrefetchScalarGridSpec(
            num_scalar_prefetch=1,
            grid=(1,),
            in_specs=[HELD] * (2 + len(arrays)),
            out_specs=out_specs,
            scratch_shapes=[
                pltpu.VMEM((HEAD_SIZE, total), jnp.bfloat16),
                pltpu.VMEM((HEAD_SIZE + 8, total), jnp.float32),
                pltpu.VMEM((1, total), jnp.float32),
                pltpu.VMEM((BLOCK, total), jnp.float32),
                pltpu.VMEM((1, total), jnp.float32),
            ],
        ),
        compiler_params=pltpu.CompilerParams(vmem_limit_bytes=20 * MIB),
        cost_estimate=pl.CostEstimate(
            flops=4 * GROUP * sum(tokens) * BLOCKS * BLOCK * HEAD_SIZE,
            bytes_accessed=8 * MIB,
            transcendentals=GROUP * sum(tokens) * BLOCKS * BLOCK,
        ),
    )(info, *queries, *arrays)


def output_kernel(info, mixed, weight, down, up, *rest, bases):
    *outs, rows = rest
    depth = mixed.shape[1]

    @pl.when(pl.program_id(0) == 0)
    def _():
        lows = jnp.dot(mixed[...], down[...], preferred_element_type=jnp.float32)
        lows = jnp.where(keep_columns(info, bases, lows.shape[1]), ADAPTER_SCALE * lows, 0.0)
        rows[:, :depth] = mixed[...]
        rows[:, depth:] = lows.astype(jnp.bfloat16)

    chunk = up.shape[1] // pl.num_programs(0)
    columns = pl.ds(pl.multiple_of(pl.program_id(0) * chunk, chunk), chunk)
    weights = jnp.concatenate([weight[:, columns], up[:, columns]], axis=0)
    result = jnp.dot(rows[...], weights, preferred_element_type=jnp.float32).astype(jnp.bfloat16)
    at = 0
    for out in outs:
        out[:, columns] = result[at : at + out.shape[0]]
        at += out.shape[0]


def output(info, mixed, weight, down, up, bases, halved):
    rows = sum(((PIECE // 2,) * 2 if b in halved else (PIECE,) for b in bases), ())
    features = weight.shape[1]
    chunk = 1024
    depth = weight.shape[0] + up.shape[0]
    return pl.pallas_call(
        functools.partial(output_kernel, bases=bases),
        out_shape=tuple(jax.ShapeDtypeStruct((n, features), jnp.bfloat16) for n in rows),
        grid_spec=pltpu.PrefetchScalarGridSpec(
            num_scalar_prefetch=1,
            grid=(features // chunk,),
            in_specs=[HELD] * 4,
            out_specs=(HELD,) * len(rows),
            scratch_shapes=[pltpu.VMEM((mixed.shape[0], depth), jnp.bfloat16)],
        ),
        compiler_params=pltpu.CompilerParams(vmem_limit_bytes=12 * MIB),
        cost_estimate=pl.CostEstimate(
            flops=2 * mixed.shape[0] * depth * features,
            bytes_accessed=2 * features * (depth + mixed.shape[0]),
            transcendentals=0,
        ),
    )(info, mixed, weight, down, up)


def normalize_kernel(activations, gain, out, top, end):
    half = top.shape[0]
    step = pl.program_id(0)
    values = activations[...].astype(jnp.float32)
    power = jnp.mean(values * values, axis=1, keepdims=True)
    normed = (values * lax.rsqrt(power + EPS_NORM) * gain[...]).astype(jnp.bfloat16)
    out[pl.ds(pl.multiple_of(step * half, half), half)] = normed

    @pl.when(step == 0)
    def _():
        top[...] = normed

    @pl.when(step == 1)
    def _():
        end[...] = normed


def normalize(activations, input_norm_gain):
    rows, features = activations.shape
    half = rows // 2
    shape = lambda n: jax.ShapeDtypeStruct((n, features), jnp.bfloat16)
    return pl.pallas_call(
        normalize_kernel,
        out_shape=(shape(rows), shape(half), shape(half)),
        grid=(2,),
        in_specs=[
            pl.BlockSpec((half, features), lambda i: (i, 0)),
            pl.BlockSpec((1, features), lambda i: (0, 0)),
        ],
        out_specs=(HELD,) * 3,
        compiler_params=pltpu.CompilerParams(vmem_limit_bytes=58 * MIB),
    )(activations, input_norm_gain[None, :])


def along_y(rows, hop):
    return lax.ppermute(
        rows, "uly", [(z * 4 + y, z * 4 + (y + hop) % 4) for z in range(2) for y in range(4)]
    )


def across_z(rows):
    pairs = [(b * 8 + u, (b ^ OTHER) * 8 + (u ^ 4)) for b in range(16) for u in range(8)]
    return lax.ppermute(rows, ("blk", "uly"), pairs)


def flipped(rows, bit):
    return lax.ppermute(rows, "blk", [(b, b ^ bit) for b in range(16)])


def along_x(rows, hop):
    return lax.ppermute(rows, "blk", [(b, (b + 4 * hop) % 16) for b in range(16)])


def in_steps(kv, other, from_m, from_p, far):
    other_m, other_p, other_far = along_x(other, 1), along_x(other, -1), flipped(far, 2)
    return [
        (0, 0, 0, kv),
        (3, 0, 0, from_m),
        (1, 0, 0, from_p),
        (2, 0, 0, far),
        (0, 1, 0, other),
        (3, 1, 0, other_m),
        (1, 1, 0, other_p),
        (2, 1, 0, other_far),
    ]


def both_cores(found):
    return [(dx, dz, 0, at, a) for dx, dz, at, a in found] + [
        (dx, dz, 1, at, flipped(a, 1)) for dx, dz, at, a in found
    ]


def plan(segment_index, segment_adapter):
    block, head = lax.axis_index("blk"), lax.axis_index("uly")
    z, y = head // 4, head % 4
    ys = [y, (y + 3) % 4, (y + 1) % 4, (y + 2) % 4]
    here = [z * 4 + p for p in ys]
    there = [(1 - z) * 4 + p for p in ys]
    firsts = [block * BLOCK + p * PIECE for p in here]
    firsts += [(block ^ OTHER) * BLOCK + p * PIECE for p in there]
    ends = jnp.sum(
        segment_index[None, :] < jnp.arange(1, 4, dtype=jnp.int32)[:, None], axis=1, dtype=jnp.int32
    )
    return jnp.concatenate(
        [
            jnp.stack(firsts).astype(jnp.int32),
            ends,
            segment_adapter,
            jnp.stack(here + there).astype(jnp.int32),
            jnp.stack([block // 4, (block // 2) % 2, block % 2]).astype(jnp.int32),
        ]
    )


def added(*terms):
    return sum(t.astype(jnp.float32) for t in terms).astype(jnp.bfloat16)


def shards(
    activations,
    input_norm_gain,
    query_weight,
    key_weight,
    value_weight,
    output_weight,
    adapter_down_maps,
    query_up_maps,
    key_up_maps,
    value_up_maps,
    output_down_maps,
    output_up_maps,
    segment_index,
    segment_adapter,
):
    info = plan(segment_index, segment_adapter)
    mid = PIECE // 2
    own, own_top, own_end = normalize(activations, input_norm_gain)
    m_top, p_end, other = along_y(own_top, 1), along_y(own_end, -1), across_z(own)
    m_end, p_top = along_y(own_end, 1), along_y(own_top, -1)
    far_top, far_end = along_y(m_top, 1), along_y(p_end, -1)
    other_m, other_p = along_y(other, 1), along_y(other, -1)
    other_far = across_z(jnp.concatenate([far_top, far_end], axis=0))

    down = adapter_down_maps
    kv_weights, kv_ups = (key_weight, value_weight), (key_up_maps, value_up_maps)
    rows1 = [own, m_top, m_end, p_top, p_end, other]
    rows2 = [far_top, far_end, other_m, other_p, other_far]
    kv = project(info, rows1, CHUNKS[:4], down, (1, 2), kv_weights, kv_ups)
    q_operands = (down, (0,), (query_weight,), (query_up_maps,))
    q1 = project(info, rows1, CHUNKS[:4], *q_operands)
    kv, q1 = lax.optimization_barrier((kv, q1))
    kv = project(info, rows2, CHUNKS[4:], down, (1, 2), kv_weights, kv_ups, before=(kv,))
    steps = flipped(kv, 2), along_x(kv, 1), along_x(kv, -1), along_x(kv, 2)
    q2 = project(info, rows2, CHUNKS[4:], *q_operands)
    other, q2 = lax.optimization_barrier((steps[0], q2))
    steps = (other, *steps[1:])
    shares = both_cores(in_steps(kv, *steps))
    queries = (q1, q2)

    def products(mixed, bases, halved=()):
        weights = output_weight, output_down_maps, output_up_maps
        return output(info, mixed, *weights, bases, halved)

    mixed, kv = attend(info, queries, ((7, 5, 6),), shares)
    bf, bm, bp = products(mixed, (7, 5, 6))
    for_far, from_m, from_p = across_z(bf), along_y(bp, 1), along_y(bm, -1)
    mixed = attend(info, queries, ((3, 1, 2), (4,)), kv=kv)
    af, am_top, am_end, ap_top, ap_end, b0 = products(mixed, (3, 1, 2, 4), halved=(1, 2))
    from_m_end, from_p_top = along_y(ap_end, 1), along_y(am_top, -1)
    far = added(af, for_far)
    other_sum = added(b0, from_m, from_p)
    queries, far, other_sum = lax.optimization_barrier((queries, far, other_sum))
    top, end = along_y(far[:mid], 1), along_y(far[mid:], -1)
    for_own = across_z(other_sum)
    to_p, to_m = added(ap_top, top), added(am_end, end)
    to_p, to_m, from_m_end, from_p_top = lax.optimization_barrier((to_p, to_m, from_m_end, from_p_top))
    from_m_top, from_p_end = along_y(to_p, 1), along_y(to_m, -1)
    (a0,) = products(attend(info, queries, ((0,),), kv=kv), (0,))
    from_m = jnp.concatenate([from_m_top, from_m_end], axis=0)
    from_p = jnp.concatenate([from_p_top, from_p_end], axis=0)
    return added(a0, from_m, from_p, for_own)


def solution(mesh):
    return jax.shard_map(
        shards,
        mesh=mesh,
        in_specs=(
            P(("blk", "uly"), None),
            P(),
            P(None, "uly"),
            P(None, "uly"),
            P(None, "uly"),
            P("uly", None),
            P(),
            P(None, "uly"),
            P(None, "uly"),
            P(None, "uly"),
            P("uly", None),
            P(),
            P(),
            P(),
        ),
        out_specs=P(("blk", "uly"), None),
        check_vma=False,
    )
```

```python
import functools
import math

import jax
import jax.numpy as jnp
from jax import lax
from jax.experimental import pallas as pl
from jax.experimental.pallas import tpu as pltpu
from jax.sharding import PartitionSpec as P

HEAD_SIZE = 128
ADAPTER_RANK = 16
ADAPTER_COUNT = 8
GROUP = 4
PIECE = 96
HALF = 384
BLOCK = 768
BLOCKS = 16
OTHER = 2
EPS_NORM = 1e-05
ADAPTER_SCALE = 2.0
MASKED = -1e30
LEAST = -1e20
EXP2_SCALE = math.log2(math.e) / math.sqrt(HEAD_SIZE)
MIB = 2**20
HELD = pl.BlockSpec(memory_space=pltpu.VMEM)
UNIT = 48
CHUNKS = (0, 1, 2, 5, 6, 7, 8, 9, 3, 4, 10, 11, 12, 13, 14, 15)
HALF_CHUNKS = len(CHUNKS) // 2
HELD = pl.BlockSpec(memory_space=pltpu.VMEM)
WIDTH = 512

INFO = 26


def halves_of(pieces):
    return sum(((2 * p, 2 * p + 1) for p in pieces), ())


def pos_of(info, halves):
    index = lax.broadcasted_iota(jnp.int32, (UNIT * len(halves), 1), 0)
    pos = index
    for i, half in enumerate(halves):
        start = info[half // 2] + half % 2 * UNIT
        pos = jnp.where(index >= i * UNIT, index + (start - i * UNIT), pos)
    return pos


def start_of(info, pos):
    start = jnp.zeros_like(pos)
    for s in range(8, 11):
        start = jnp.where(pos >= info[s], info[s], start)
    return start


def tenant_of(info, pos):
    tenant = jnp.zeros_like(pos) + info[11]
    for s in range(3):
        tenant = jnp.where(pos >= info[8 + s], info[12 + s], tenant)
    return tenant


def keep_columns(info, halves, columns):
    tenant = tenant_of(info, pos_of(info, halves))
    column = lax.broadcasted_iota(jnp.int32, (len(halves) * UNIT, columns), 1)
    return (column // ADAPTER_RANK) % ADAPTER_COUNT == tenant


def project_kernel(info, *refs, halves, parts, targets, earlier):
    rows, refs = refs[:parts], refs[parts:]
    if earlier:
        before, refs = refs[0], refs[1:]
    down, weights, ups = refs[0], refs[1 : 1 + len(targets)], refs[1 + len(targets) : -2]
    out, acc = refs[-2:]
    step = pl.program_id(0)
    hidden = ADAPTER_COUNT * ADAPTER_RANK
    chunk = down.shape[0] // pl.num_programs(0)
    columns = pl.ds(pl.multiple_of(step * chunk, chunk), chunk)
    x = jnp.concatenate([r[:, columns] for r in rows], axis=0)
    w = [w[columns] for w in weights]
    w += [down[columns, t * hidden : (t + 1) * hidden] for t in targets]
    product = jnp.dot(x, jnp.concatenate(w, axis=1), preferred_element_type=jnp.float32)

    @pl.when(step == 0)
    def _():
        acc[...] = product

    @pl.when(step > 0)
    def _():
        acc[...] += product

    @pl.when(step == pl.num_programs(0) - 1)
    def _():
        keep = keep_columns(info, halves, hidden)
        new = 0
        if earlier:
            new = before.shape[0]
            out[:new] = before[...]
        at, low_at = 0, out.shape[1]
        for weight, up in zip(weights, ups):
            width = weight.shape[1]
            low = jnp.where(keep, acc[:, low_at : low_at + hidden], 0.0).astype(jnp.bfloat16)
            adapted = jnp.dot(low, up[...], preferred_element_type=jnp.float32)
            out[new:, at : at + width] = (
                acc[:, at : at + width] + ADAPTER_SCALE * adapted
            ).astype(jnp.bfloat16)
            at += width
            low_at += hidden


def project(info, rows, halves, down, targets, weights, ups, before=()):
    depth, count = down.shape[0], sum(r.shape[0] for r in rows)
    width = sum(w.shape[1] for w in weights)
    wide = width + ADAPTER_COUNT * ADAPTER_RANK * len(targets)
    return pl.pallas_call(
        functools.partial(
            project_kernel,
            halves=halves,
            parts=len(rows),
            targets=targets,
            earlier=bool(before),
        ),
        out_shape=jax.ShapeDtypeStruct((count + sum(b.shape[0] for b in before), width), jnp.bfloat16),
        grid_spec=pltpu.PrefetchScalarGridSpec(
            num_scalar_prefetch=1,
            grid=(depth // 1024,),
            in_specs=[HELD] * (len(rows) + len(before) + 1 + 2 * len(targets)),
            out_specs=HELD,
            scratch_shapes=[pltpu.VMEM((count, wide), jnp.float32)],
        ),
        compiler_params=pltpu.CompilerParams(vmem_limit_bytes=14 * MIB),
        cost_estimate=pl.CostEstimate(
            flops=4 * count * depth * wide,
            bytes_accessed=2 * depth * (wide + count),
            transcendentals=0,
        ),
    )(info, *rows, *before, down, *weights, *ups)


def positions(info, bases):
    tokens = len(bases) * PIECE
    column = lax.broadcasted_iota(jnp.int32, (1, GROUP * tokens), 1)
    pos = column
    for h in range(GROUP):
        for i, base in enumerate(bases):
            at = h * tokens + i * PIECE
            pos = jnp.where(column >= at, column + (info[base] - at), pos)
    return pos


def attend_kernel(info, q1, q2, *refs, sections, parts):
    shares, refs = refs[: len(parts)], refs[len(parts) :]
    if parts:
        out, kv, qt, acc, peak, held, held_peak = refs
    else:
        kv, out, qt, acc, peak, held, held_peak = refs
    for ref, (dx, dz, dc, at) in zip(shares, parts):
        x = lax.rem(info[23] + dx, 4)
        z = info[24] if dz == 0 else 1 - info[24]
        c = info[25] if dc == 0 else 1 - info[25]
        kv[x * 4 + z * 2 + c, at : at + ref.shape[0]] = ref[...]
    index = lax.broadcasted_iota(jnp.int32, (BLOCK, 1), 0)
    offsets = index
    for i, half in enumerate(CHUNKS):
        start = info[15 + half // 2] * PIECE + half % 2 * UNIT
        offsets = jnp.where(index >= i * UNIT, index + (start - i * UNIT), offsets)

    def of_block(t, at):
        here = lambda i: CHUNKS[i] < 8
        spans, i = [], 0
        while i < len(CHUNKS):
            n = 1
            while i + n < len(CHUNKS) and here(i + n) == here(i):
                n += 1
            device = t if here(i) else t ^ OTHER
            spans.append(kv[device, i * UNIT : (i + n) * UNIT, at : at + HEAD_SIZE])
            i += n
        return jnp.concatenate(spans, axis=0)

    done = 0
    for pieces in sections:
        tokens = len(pieces) * PIECE
        total = GROUP * tokens
        width = WIDTH if total % WIDTH == 0 else PIECE * GROUP
        rows = []
        for half in halves_of(pieces):
            place = CHUNKS.index(half)
            ref, place = (q1, place) if place < HALF_CHUNKS else (q2, place - HALF_CHUNKS)
            rows.append(ref[place * UNIT : (place + 1) * UNIT])
        q = jnp.concatenate(rows, axis=0)
        q = [q[:, h * HEAD_SIZE : (h + 1) * HEAD_SIZE] for h in range(GROUP)]
        qt[:, :total] = jnp.concatenate(q, axis=0).T
        acc[:, :total] = jnp.zeros((HEAD_SIZE + 8, total), jnp.float32)
        peak[:, :total] = jnp.full((1, total), LEAST, jnp.float32)
        pos = positions(info, pieces)
        low = start_of(info, pos)
        first = last = info[pieces[0]]
        for piece in pieces[1:]:
            first, last = jnp.minimum(first, info[piece]), jnp.maximum(last, info[piece])
        last = last + (PIECE - 1)
        n0 = start_of(info, first) // BLOCK
        own = first // BLOCK
        m1 = jnp.clip((start_of(info, last) + BLOCK - 1) // BLOCK, n0, own)

        def step(now, later, causal=False, starts=False):
            if later is not None:
                keys = of_block(later, 0)
            if now is not None:
                values = jnp.concatenate(
                    [of_block(now, HEAD_SIZE).T, jnp.ones((8, BLOCK), jnp.bfloat16)], axis=0
                )
            for c in range(0, total, width):
                at = slice(c, c + width)
                if now is not None:
                    old = peak[:, at]
                    fresh = jnp.maximum(old, held_peak[:, at])
                    weights = jnp.exp2((held[:, at] - fresh) * EXP2_SCALE).astype(jnp.bfloat16)
                    decay = jnp.exp2((old - fresh) * EXP2_SCALE)
                    peak[:, at] = fresh
                if later is not None:
                    scores = jnp.dot(keys, qt[:, at], preferred_element_type=jnp.float32)
                    if causal or starts:
                        key_pos = offsets + later * BLOCK
                        allowed = key_pos >= low[:, at]
                        if causal:
                            allowed &= key_pos <= pos[:, at]
                        scores = jnp.where(allowed, scores, MASKED)
                    held[:, at] = scores
                    held_peak[:, at] = jnp.max(scores, axis=0, keepdims=True)
                if now is not None:
                    acc[:, at] = acc[:, at] * decay + jnp.dot(
                        values, weights, preferred_element_type=jnp.float32
                    )

        def starting_step(j, now):
            step(now, j, starts=True)
            return j

        def plain_step(j, now):
            step(now, j)
            return j

        step(None, own, causal=True)
        now = lax.fori_loop(n0, m1, starting_step, own)
        now = lax.fori_loop(m1, own, plain_step, now)
        step(now, None)
        mixed = acc[:HEAD_SIZE, :total] / acc[HEAD_SIZE : HEAD_SIZE + 1, :total]
        mixed = mixed.T.astype(jnp.bfloat16)
        for h in range(GROUP):
            out[done : done + tokens, h * HEAD_SIZE : (h + 1) * HEAD_SIZE] = mixed[
                h * tokens : (h + 1) * tokens
            ]
        done += tokens


def attend(info, queries, sections, shares=(), kv=None):
    parts = [k[:4] for k in shares]
    arrays = [k[4] for k in shares] if kv is None else [kv]
    tokens = [len(s) * PIECE for s in sections]
    total = GROUP * max(tokens)
    out_shape = jax.ShapeDtypeStruct((sum(tokens), GROUP * HEAD_SIZE), jnp.bfloat16)
    out_specs = pl.BlockSpec(out_shape.shape, lambda i, s: (0, 0))
    if kv is None:
        out_shape = (out_shape, jax.ShapeDtypeStruct((BLOCKS, BLOCK, 2 * HEAD_SIZE), jnp.bfloat16))
        out_specs = (out_specs, HELD)
    return pl.pallas_call(
        functools.partial(attend_kernel, sections=sections, parts=parts),
        out_shape=out_shape,
        grid_spec=pltpu.PrefetchScalarGridSpec(
            num_scalar_prefetch=1,
            grid=(1,),
            in_specs=[HELD] * (2 + len(arrays)),
            out_specs=out_specs,
            scratch_shapes=[
                pltpu.VMEM((HEAD_SIZE, total), jnp.bfloat16),
                pltpu.VMEM((HEAD_SIZE + 8, total), jnp.float32),
                pltpu.VMEM((1, total), jnp.float32),
                pltpu.VMEM((BLOCK, total), jnp.float32),
                pltpu.VMEM((1, total), jnp.float32),
            ],
        ),
        compiler_params=pltpu.CompilerParams(vmem_limit_bytes=20 * MIB),
        cost_estimate=pl.CostEstimate(
            flops=4 * GROUP * sum(tokens) * BLOCKS * BLOCK * HEAD_SIZE,
            bytes_accessed=8 * MIB,
            transcendentals=GROUP * sum(tokens) * BLOCKS * BLOCK,
        ),
    )(info, *queries, *arrays)


def output_kernel(info, mixed, weight, down, up, *rest, bases):
    *outs, rows = rest
    depth = mixed.shape[1]

    @pl.when(pl.program_id(0) == 0)
    def _():
        lows = jnp.dot(mixed[...], down[...], preferred_element_type=jnp.float32)
        lows = jnp.where(keep_columns(info, halves_of(bases), lows.shape[1]), ADAPTER_SCALE * lows, 0.0)
        rows[:, :depth] = mixed[...]
        rows[:, depth:] = lows.astype(jnp.bfloat16)

    chunk = up.shape[1] // pl.num_programs(0)
    columns = pl.ds(pl.multiple_of(pl.program_id(0) * chunk, chunk), chunk)
    weights = jnp.concatenate([weight[:, columns], up[:, columns]], axis=0)
    result = jnp.dot(rows[...], weights, preferred_element_type=jnp.float32).astype(jnp.bfloat16)
    at = 0
    for out in outs:
        out[:, columns] = result[at : at + out.shape[0]]
        at += out.shape[0]


def output(info, mixed, weight, down, up, bases, halved):
    rows = sum(((PIECE // 2,) * 2 if b in halved else (PIECE,) for b in bases), ())
    features = weight.shape[1]
    chunk = 1024
    depth = weight.shape[0] + up.shape[0]
    return pl.pallas_call(
        functools.partial(output_kernel, bases=bases),
        out_shape=tuple(jax.ShapeDtypeStruct((n, features), jnp.bfloat16) for n in rows),
        grid_spec=pltpu.PrefetchScalarGridSpec(
            num_scalar_prefetch=1,
            grid=(features // chunk,),
            in_specs=[HELD] * 4,
            out_specs=(HELD,) * len(rows),
            scratch_shapes=[pltpu.VMEM((mixed.shape[0], depth), jnp.bfloat16)],
        ),
        compiler_params=pltpu.CompilerParams(vmem_limit_bytes=12 * MIB),
        cost_estimate=pl.CostEstimate(
            flops=2 * mixed.shape[0] * depth * features,
            bytes_accessed=2 * features * (depth + mixed.shape[0]),
            transcendentals=0,
        ),
    )(info, mixed, weight, down, up)


def normalize_kernel(activations, gain, out, top, end):
    half = top.shape[0]
    step = pl.program_id(0)
    values = activations[...].astype(jnp.float32)
    power = jnp.mean(values * values, axis=1, keepdims=True)
    normed = (values * lax.rsqrt(power + EPS_NORM) * gain[...]).astype(jnp.bfloat16)
    out[pl.ds(pl.multiple_of(step * half, half), half)] = normed

    @pl.when(step == 0)
    def _():
        top[...] = normed

    @pl.when(step == 1)
    def _():
        end[...] = normed


def normalize(activations, input_norm_gain):
    rows, features = activations.shape
    half = rows // 2
    shape = lambda n: jax.ShapeDtypeStruct((n, features), jnp.bfloat16)
    return pl.pallas_call(
        normalize_kernel,
        out_shape=(shape(rows), shape(half), shape(half)),
        grid=(2,),
        in_specs=[
            pl.BlockSpec((half, features), lambda i: (i, 0)),
            pl.BlockSpec((1, features), lambda i: (0, 0)),
        ],
        out_specs=(HELD,) * 3,
        compiler_params=pltpu.CompilerParams(vmem_limit_bytes=58 * MIB),
    )(activations, input_norm_gain[None, :])


def along_y(rows, hop):
    return lax.ppermute(
        rows, "uly", [(z * 4 + y, z * 4 + (y + hop) % 4) for z in range(2) for y in range(4)]
    )


def across_z(rows):
    pairs = [(b * 8 + u, (b ^ OTHER) * 8 + (u ^ 4)) for b in range(16) for u in range(8)]
    return lax.ppermute(rows, ("blk", "uly"), pairs)


def flipped(rows, bit):
    return lax.ppermute(rows, "blk", [(b, b ^ bit) for b in range(16)])


def along_x(rows, hop):
    return lax.ppermute(rows, "blk", [(b, (b + 4 * hop) % 16) for b in range(16)])


def in_steps(kv, other, from_m, from_p, far):
    other_m, other_p, other_far = along_x(other, 1), along_x(other, -1), flipped(far, 2)
    return [
        (0, 0, 0, kv),
        (3, 0, 0, from_m),
        (1, 0, 0, from_p),
        (2, 0, 0, far),
        (0, 1, 0, other),
        (3, 1, 0, other_m),
        (1, 1, 0, other_p),
        (2, 1, 0, other_far),
    ]


def both_cores(found):
    return [(dx, dz, 0, at, a) for dx, dz, at, a in found] + [
        (dx, dz, 1, at, flipped(a, 1)) for dx, dz, at, a in found
    ]


def plan(segment_index, segment_adapter):
    block, head = lax.axis_index("blk"), lax.axis_index("uly")
    z, y = head // 4, head % 4
    ys = [y, (y + 3) % 4, (y + 1) % 4, (y + 2) % 4]
    here = [z * 4 + p for p in ys]
    there = [(1 - z) * 4 + p for p in ys]
    firsts = [block * BLOCK + p * PIECE for p in here]
    firsts += [(block ^ OTHER) * BLOCK + p * PIECE for p in there]
    ends = jnp.sum(
        segment_index[None, :] < jnp.arange(1, 4, dtype=jnp.int32)[:, None], axis=1, dtype=jnp.int32
    )
    return jnp.concatenate(
        [
            jnp.stack(firsts).astype(jnp.int32),
            ends,
            segment_adapter,
            jnp.stack(here + there).astype(jnp.int32),
            jnp.stack([block // 4, (block // 2) % 2, block % 2]).astype(jnp.int32),
        ]
    )


def added(*terms):
    return sum(t.astype(jnp.float32) for t in terms).astype(jnp.bfloat16)


def shards(
    activations,
    input_norm_gain,
    query_weight,
    key_weight,
    value_weight,
    output_weight,
    adapter_down_maps,
    query_up_maps,
    key_up_maps,
    value_up_maps,
    output_down_maps,
    output_up_maps,
    segment_index,
    segment_adapter,
):
    info = plan(segment_index, segment_adapter)
    mid = PIECE // 2
    own, own_top, own_end = normalize(activations, input_norm_gain)
    m_top, p_end, other = along_y(own_top, 1), along_y(own_end, -1), across_z(own)
    own_top, own_end, other = lax.optimization_barrier((own_top, own_end, other))
    m_end, p_top = along_y(own_end, 1), along_y(own_top, -1)
    far_top, far_end = along_y(m_top, 1), along_y(p_end, -1)
    other_m, other_p = along_y(other, 1), along_y(other, -1)
    other_far = across_z(jnp.concatenate([far_top, far_end], axis=0))

    down = adapter_down_maps
    kv_weights, kv_ups = (key_weight, value_weight), (key_up_maps, value_up_maps)
    rows1 = [own, m_top, p_end, far_top, far_end, other]
    rows2 = [m_end, p_top, other_m, other_p, other_far]
    kv = project(info, rows1, CHUNKS[:HALF_CHUNKS], down, (1, 2), kv_weights, kv_ups)
    q_operands = (down, (0,), (query_weight,), (query_up_maps,))
    q1 = project(info, rows1, CHUNKS[:HALF_CHUNKS], *q_operands)
    kv, q1 = lax.optimization_barrier((kv, q1))
    kv = project(info, rows2, CHUNKS[HALF_CHUNKS:], down, (1, 2), kv_weights, kv_ups, before=(kv,))
    steps = flipped(kv, 2), along_x(kv, 1), along_x(kv, -1), along_x(kv, 2)
    q2 = project(info, rows2, CHUNKS[HALF_CHUNKS:], *q_operands)
    other, q2 = lax.optimization_barrier((steps[0], q2))
    steps = (other, *steps[1:])
    shares = both_cores(in_steps(kv, *steps))
    queries = (q1, q2)

    def products(mixed, bases, halved=()):
        weights = output_weight, output_down_maps, output_up_maps
        return output(info, mixed, *weights, bases, halved)

    mixed, kv = attend(info, queries, ((7, 5, 6),), shares)
    bf, bm, bp = products(mixed, (7, 5, 6))
    for_far, from_m, from_p = across_z(bf), along_y(bp, 1), along_y(bm, -1)
    mixed = attend(info, queries, ((3, 1, 2), (4,)), kv=kv)
    af, am_top, am_end, ap_top, ap_end, b0 = products(mixed, (3, 1, 2, 4), halved=(1, 2))
    from_m_end, from_p_top = along_y(ap_end, 1), along_y(am_top, -1)
    far = added(af, for_far)
    other_sum = added(b0, from_m, from_p)
    queries, far, other_sum = lax.optimization_barrier((queries, far, other_sum))
    top, end = along_y(far[:mid], 1), along_y(far[mid:], -1)
    for_own = across_z(other_sum)
    to_p, to_m = added(ap_top, top), added(am_end, end)
    from_m_top, from_p_end = along_y(to_p, 1), along_y(to_m, -1)
    (a0,) = products(attend(info, queries, ((0,),), kv=kv), (0,))
    late = jnp.concatenate([from_m_top, from_p_end], axis=0)
    early = jnp.concatenate([from_p_top, from_m_end], axis=0)
    return added(late, early, for_own, a0)


def solution(mesh):
    return jax.shard_map(
        shards,
        mesh=mesh,
        in_specs=(
            P(("blk", "uly"), None),
            P(),
            P(None, "uly"),
            P(None, "uly"),
            P(None, "uly"),
            P("uly", None),
            P(),
            P(None, "uly"),
            P(None, "uly"),
            P(None, "uly"),
            P("uly", None),
            P(),
            P(),
            P(),
        ),
        out_specs=P(("blk", "uly"), None),
        check_vma=False,
    )
```

```python
import functools
import math

import jax
import jax.numpy as jnp
from jax import lax
from jax.experimental import pallas as pl
from jax.experimental.pallas import tpu as pltpu
from jax.sharding import PartitionSpec as P

HEAD_SIZE = 128
ADAPTER_RANK = 16
ADAPTER_COUNT = 8
GROUP = 4
PIECE = 96
HALF = 384
BLOCK = 768
BLOCKS = 16
OTHER = 2
EPS_NORM = 1e-05
ADAPTER_SCALE = 2.0
MASKED = -1e30
LEAST = -1e20
EXP2_SCALE = math.log2(math.e) / math.sqrt(HEAD_SIZE)
MIB = 2**20
HELD = pl.BlockSpec(memory_space=pltpu.VMEM)
UNIT = 48
CHUNKS = (0, 1, 2, 5, 6, 7, 8, 9, 3, 4, 10, 11, 12, 13, 14, 15)
HALF_CHUNKS = len(CHUNKS) // 2
HELD = pl.BlockSpec(memory_space=pltpu.VMEM)
WIDTH = 512

INFO = 26


def halves_of(pieces):
    return sum(((2 * p, 2 * p + 1) for p in pieces), ())


def pos_of(info, halves):
    index = lax.broadcasted_iota(jnp.int32, (UNIT * len(halves), 1), 0)
    pos = index
    for i, half in enumerate(halves):
        start = info[half // 2] + half % 2 * UNIT
        pos = jnp.where(index >= i * UNIT, index + (start - i * UNIT), pos)
    return pos


def start_of(info, pos):
    start = jnp.zeros_like(pos)
    for s in range(8, 11):
        start = jnp.where(pos >= info[s], info[s], start)
    return start


def tenant_of(info, pos):
    tenant = jnp.zeros_like(pos) + info[11]
    for s in range(3):
        tenant = jnp.where(pos >= info[8 + s], info[12 + s], tenant)
    return tenant


def keep_columns(info, halves, columns):
    tenant = tenant_of(info, pos_of(info, halves))
    column = lax.broadcasted_iota(jnp.int32, (len(halves) * UNIT, columns), 1)
    return (column // ADAPTER_RANK) % ADAPTER_COUNT == tenant


def project_kernel(info, *refs, halves, parts, targets, earlier):
    rows, refs = refs[:parts], refs[parts:]
    if earlier:
        before, refs = refs[0], refs[1:]
    down, weights, ups = refs[0], refs[1 : 1 + len(targets)], refs[1 + len(targets) : -2]
    out, acc = refs[-2:]
    step = pl.program_id(0)
    hidden = ADAPTER_COUNT * ADAPTER_RANK
    chunk = down.shape[0] // pl.num_programs(0)
    columns = pl.ds(pl.multiple_of(step * chunk, chunk), chunk)
    x = jnp.concatenate([r[:, columns] for r in rows], axis=0)
    w = [w[columns] for w in weights]
    w += [down[columns, t * hidden : (t + 1) * hidden] for t in targets]
    product = jnp.dot(x, jnp.concatenate(w, axis=1), preferred_element_type=jnp.float32)

    @pl.when(step == 0)
    def _():
        acc[...] = product

    @pl.when(step > 0)
    def _():
        acc[...] += product

    @pl.when(step == pl.num_programs(0) - 1)
    def _():
        keep = keep_columns(info, halves, hidden)
        new = 0
        if earlier:
            new = before.shape[0]
            out[:new] = before[...]
        at, low_at = 0, out.shape[1]
        for weight, up in zip(weights, ups):
            width = weight.shape[1]
            low = jnp.where(keep, acc[:, low_at : low_at + hidden], 0.0).astype(jnp.bfloat16)
            adapted = jnp.dot(low, up[...], preferred_element_type=jnp.float32)
            out[new:, at : at + width] = (
                acc[:, at : at + width] + ADAPTER_SCALE * adapted
            ).astype(jnp.bfloat16)
            at += width
            low_at += hidden


def project(info, rows, halves, down, targets, weights, ups, before=()):
    depth, count = down.shape[0], sum(r.shape[0] for r in rows)
    width = sum(w.shape[1] for w in weights)
    wide = width + ADAPTER_COUNT * ADAPTER_RANK * len(targets)
    return pl.pallas_call(
        functools.partial(
            project_kernel,
            halves=halves,
            parts=len(rows),
            targets=targets,
            earlier=bool(before),
        ),
        out_shape=jax.ShapeDtypeStruct((count + sum(b.shape[0] for b in before), width), jnp.bfloat16),
        grid_spec=pltpu.PrefetchScalarGridSpec(
            num_scalar_prefetch=1,
            grid=(1,),
            in_specs=[HELD] * (len(rows) + len(before) + 1 + 2 * len(targets)),
            out_specs=HELD,
            scratch_shapes=[pltpu.VMEM((count, wide), jnp.float32)],
        ),
        compiler_params=pltpu.CompilerParams(vmem_limit_bytes=24 * MIB),
        cost_estimate=pl.CostEstimate(
            flops=4 * count * depth * wide,
            bytes_accessed=2 * depth * (wide + count),
            transcendentals=0,
        ),
    )(info, *rows, *before, down, *weights, *ups)


def positions(info, bases):
    tokens = len(bases) * PIECE
    column = lax.broadcasted_iota(jnp.int32, (1, GROUP * tokens), 1)
    pos = column
    for h in range(GROUP):
        for i, base in enumerate(bases):
            at = h * tokens + i * PIECE
            pos = jnp.where(column >= at, column + (info[base] - at), pos)
    return pos


def attend_kernel(info, q1, q2, *refs, sections, parts):
    shares, refs = refs[: len(parts)], refs[len(parts) :]
    if parts:
        out, kv, qt, acc, peak, held, held_peak = refs
    else:
        kv, out, qt, acc, peak, held, held_peak = refs
    for ref, (dx, dz, dc, at) in zip(shares, parts):
        x = lax.rem(info[23] + dx, 4)
        z = info[24] if dz == 0 else 1 - info[24]
        c = info[25] if dc == 0 else 1 - info[25]
        kv[x * 4 + z * 2 + c, at : at + ref.shape[0]] = ref[...]
    index = lax.broadcasted_iota(jnp.int32, (BLOCK, 1), 0)
    offsets = index
    for i, half in enumerate(CHUNKS):
        start = info[15 + half // 2] * PIECE + half % 2 * UNIT
        offsets = jnp.where(index >= i * UNIT, index + (start - i * UNIT), offsets)

    def of_block(t, at):
        here = lambda i: CHUNKS[i] < 8
        spans, i = [], 0
        while i < len(CHUNKS):
            n = 1
            while i + n < len(CHUNKS) and here(i + n) == here(i):
                n += 1
            device = t if here(i) else t ^ OTHER
            spans.append(kv[device, i * UNIT : (i + n) * UNIT, at : at + HEAD_SIZE])
            i += n
        return jnp.concatenate(spans, axis=0)

    done = 0
    for pieces in sections:
        tokens = len(pieces) * PIECE
        total = GROUP * tokens
        width = WIDTH if total % WIDTH == 0 else PIECE * GROUP
        rows = []
        for half in halves_of(pieces):
            place = CHUNKS.index(half)
            ref, place = (q1, place) if place < HALF_CHUNKS else (q2, place - HALF_CHUNKS)
            rows.append(ref[place * UNIT : (place + 1) * UNIT])
        q = jnp.concatenate(rows, axis=0)
        q = [q[:, h * HEAD_SIZE : (h + 1) * HEAD_SIZE] for h in range(GROUP)]
        qt[:, :total] = jnp.concatenate(q, axis=0).T
        acc[:, :total] = jnp.zeros((HEAD_SIZE + 8, total), jnp.float32)
        peak[:, :total] = jnp.full((1, total), LEAST, jnp.float32)
        pos = positions(info, pieces)
        low = start_of(info, pos)
        first = last = info[pieces[0]]
        for piece in pieces[1:]:
            first, last = jnp.minimum(first, info[piece]), jnp.maximum(last, info[piece])
        last = last + (PIECE - 1)
        n0 = start_of(info, first) // BLOCK
        own = first // BLOCK
        m1 = jnp.clip((start_of(info, last) + BLOCK - 1) // BLOCK, n0, own)

        def step(now, later, causal=False, starts=False):
            if later is not None:
                keys = of_block(later, 0)
            if now is not None:
                values = jnp.concatenate(
                    [of_block(now, HEAD_SIZE).T, jnp.ones((8, BLOCK), jnp.bfloat16)], axis=0
                )
            for c in range(0, total, width):
                at = slice(c, c + width)
                if now is not None:
                    old = peak[:, at]
                    fresh = jnp.maximum(old, held_peak[:, at])
                    weights = jnp.exp2((held[:, at] - fresh) * EXP2_SCALE).astype(jnp.bfloat16)
                    decay = jnp.exp2((old - fresh) * EXP2_SCALE)
                    peak[:, at] = fresh
                if later is not None:
                    scores = jnp.dot(keys, qt[:, at], preferred_element_type=jnp.float32)
                    if causal or starts:
                        key_pos = offsets + later * BLOCK
                        allowed = key_pos >= low[:, at]
                        if causal:
                            allowed &= key_pos <= pos[:, at]
                        scores = jnp.where(allowed, scores, MASKED)
                    held[:, at] = scores
                    held_peak[:, at] = jnp.max(scores, axis=0, keepdims=True)
                if now is not None:
                    acc[:, at] = acc[:, at] * decay + jnp.dot(
                        values, weights, preferred_element_type=jnp.float32
                    )

        def starting_step(j, now):
            step(now, j, starts=True)
            return j

        def plain_step(j, now):
            step(now, j)
            return j

        step(None, own, causal=True)
        now = lax.fori_loop(n0, m1, starting_step, own)
        now = lax.fori_loop(m1, own, plain_step, now)
        step(now, None)
        mixed = acc[:HEAD_SIZE, :total] / acc[HEAD_SIZE : HEAD_SIZE + 1, :total]
        mixed = mixed.T.astype(jnp.bfloat16)
        for h in range(GROUP):
            out[done : done + tokens, h * HEAD_SIZE : (h + 1) * HEAD_SIZE] = mixed[
                h * tokens : (h + 1) * tokens
            ]
        done += tokens


def attend(info, queries, sections, shares=(), kv=None):
    parts = [k[:4] for k in shares]
    arrays = [k[4] for k in shares] if kv is None else [kv]
    tokens = [len(s) * PIECE for s in sections]
    total = GROUP * max(tokens)
    out_shape = jax.ShapeDtypeStruct((sum(tokens), GROUP * HEAD_SIZE), jnp.bfloat16)
    out_specs = pl.BlockSpec(out_shape.shape, lambda i, s: (0, 0))
    if kv is None:
        out_shape = (out_shape, jax.ShapeDtypeStruct((BLOCKS, BLOCK, 2 * HEAD_SIZE), jnp.bfloat16))
        out_specs = (out_specs, HELD)
    return pl.pallas_call(
        functools.partial(attend_kernel, sections=sections, parts=parts),
        out_shape=out_shape,
        grid_spec=pltpu.PrefetchScalarGridSpec(
            num_scalar_prefetch=1,
            grid=(1,),
            in_specs=[HELD] * (2 + len(arrays)),
            out_specs=out_specs,
            scratch_shapes=[
                pltpu.VMEM((HEAD_SIZE, total), jnp.bfloat16),
                pltpu.VMEM((HEAD_SIZE + 8, total), jnp.float32),
                pltpu.VMEM((1, total), jnp.float32),
                pltpu.VMEM((BLOCK, total), jnp.float32),
                pltpu.VMEM((1, total), jnp.float32),
            ],
        ),
        compiler_params=pltpu.CompilerParams(vmem_limit_bytes=20 * MIB),
        cost_estimate=pl.CostEstimate(
            flops=4 * GROUP * sum(tokens) * BLOCKS * BLOCK * HEAD_SIZE,
            bytes_accessed=8 * MIB,
            transcendentals=GROUP * sum(tokens) * BLOCKS * BLOCK,
        ),
    )(info, *queries, *arrays)


def output_kernel(info, mixed, weight, down, up, *rest, bases):
    *outs, rows = rest
    depth = mixed.shape[1]

    @pl.when(pl.program_id(0) == 0)
    def _():
        lows = jnp.dot(mixed[...], down[...], preferred_element_type=jnp.float32)
        lows = jnp.where(keep_columns(info, halves_of(bases), lows.shape[1]), ADAPTER_SCALE * lows, 0.0)
        rows[:, :depth] = mixed[...]
        rows[:, depth:] = lows.astype(jnp.bfloat16)

    chunk = up.shape[1] // pl.num_programs(0)
    columns = pl.ds(pl.multiple_of(pl.program_id(0) * chunk, chunk), chunk)
    weights = jnp.concatenate([weight[:, columns], up[:, columns]], axis=0)
    result = jnp.dot(rows[...], weights, preferred_element_type=jnp.float32).astype(jnp.bfloat16)
    at = 0
    for out in outs:
        out[:, columns] = result[at : at + out.shape[0]]
        at += out.shape[0]


def output(info, mixed, weight, down, up, bases, halved):
    rows = sum(((PIECE // 2,) * 2 if b in halved else (PIECE,) for b in bases), ())
    features = weight.shape[1]
    chunk = 4096
    depth = weight.shape[0] + up.shape[0]
    return pl.pallas_call(
        functools.partial(output_kernel, bases=bases),
        out_shape=tuple(jax.ShapeDtypeStruct((n, features), jnp.bfloat16) for n in rows),
        grid_spec=pltpu.PrefetchScalarGridSpec(
            num_scalar_prefetch=1,
            grid=(features // chunk,),
            in_specs=[HELD] * 4,
            out_specs=(HELD,) * len(rows),
            scratch_shapes=[pltpu.VMEM((mixed.shape[0], depth), jnp.bfloat16)],
        ),
        compiler_params=pltpu.CompilerParams(vmem_limit_bytes=24 * MIB),
        cost_estimate=pl.CostEstimate(
            flops=2 * mixed.shape[0] * depth * features,
            bytes_accessed=2 * features * (depth + mixed.shape[0]),
            transcendentals=0,
        ),
    )(info, mixed, weight, down, up)


def normalize_kernel(activations, gain, out, top, end):
    half = top.shape[0]
    step = pl.program_id(0)
    values = activations[...].astype(jnp.float32)
    power = jnp.mean(values * values, axis=1, keepdims=True)
    normed = (values * lax.rsqrt(power + EPS_NORM) * gain[...]).astype(jnp.bfloat16)
    out[pl.ds(pl.multiple_of(step * half, half), half)] = normed

    @pl.when(step == 0)
    def _():
        top[...] = normed

    @pl.when(step == 1)
    def _():
        end[...] = normed


def normalize(activations, input_norm_gain):
    rows, features = activations.shape
    half = rows // 2
    shape = lambda n: jax.ShapeDtypeStruct((n, features), jnp.bfloat16)
    return pl.pallas_call(
        normalize_kernel,
        out_shape=(shape(rows), shape(half), shape(half)),
        grid=(2,),
        in_specs=[
            pl.BlockSpec((half, features), lambda i: (i, 0)),
            pl.BlockSpec((1, features), lambda i: (0, 0)),
        ],
        out_specs=(HELD,) * 3,
        compiler_params=pltpu.CompilerParams(vmem_limit_bytes=58 * MIB),
    )(activations, input_norm_gain[None, :])


def along_y(rows, hop):
    return lax.ppermute(
        rows, "uly", [(z * 4 + y, z * 4 + (y + hop) % 4) for z in range(2) for y in range(4)]
    )


def across_z(rows):
    pairs = [(b * 8 + u, (b ^ OTHER) * 8 + (u ^ 4)) for b in range(16) for u in range(8)]
    return lax.ppermute(rows, ("blk", "uly"), pairs)


def flipped(rows, bit):
    return lax.ppermute(rows, "blk", [(b, b ^ bit) for b in range(16)])


def along_x(rows, hop):
    return lax.ppermute(rows, "blk", [(b, (b + 4 * hop) % 16) for b in range(16)])


def in_steps(kv, other, from_m, from_p, far):
    other_m, other_p, other_far = along_x(other, 1), along_x(other, -1), flipped(far, 2)
    return [
        (0, 0, 0, kv),
        (3, 0, 0, from_m),
        (1, 0, 0, from_p),
        (2, 0, 0, far),
        (0, 1, 0, other),
        (3, 1, 0, other_m),
        (1, 1, 0, other_p),
        (2, 1, 0, other_far),
    ]


def both_cores(found):
    return [(dx, dz, 0, at, a) for dx, dz, at, a in found] + [
        (dx, dz, 1, at, flipped(a, 1)) for dx, dz, at, a in found
    ]


def plan(segment_index, segment_adapter):
    block, head = lax.axis_index("blk"), lax.axis_index("uly")
    z, y = head // 4, head % 4
    ys = [y, (y + 3) % 4, (y + 1) % 4, (y + 2) % 4]
    here = [z * 4 + p for p in ys]
    there = [(1 - z) * 4 + p for p in ys]
    firsts = [block * BLOCK + p * PIECE for p in here]
    firsts += [(block ^ OTHER) * BLOCK + p * PIECE for p in there]
    ends = jnp.sum(
        segment_index[None, :] < jnp.arange(1, 4, dtype=jnp.int32)[:, None], axis=1, dtype=jnp.int32
    )
    return jnp.concatenate(
        [
            jnp.stack(firsts).astype(jnp.int32),
            ends,
            segment_adapter,
            jnp.stack(here + there).astype(jnp.int32),
            jnp.stack([block // 4, (block // 2) % 2, block % 2]).astype(jnp.int32),
        ]
    )


def added(*terms):
    return sum(t.astype(jnp.float32) for t in terms).astype(jnp.bfloat16)


def shards(
    activations,
    input_norm_gain,
    query_weight,
    key_weight,
    value_weight,
    output_weight,
    adapter_down_maps,
    query_up_maps,
    key_up_maps,
    value_up_maps,
    output_down_maps,
    output_up_maps,
    segment_index,
    segment_adapter,
):
    info = plan(segment_index, segment_adapter)
    mid = PIECE // 2
    own, own_top, own_end = normalize(activations, input_norm_gain)
    m_top, p_end, other = along_y(own_top, 1), along_y(own_end, -1), across_z(own)
    own_top, own_end, other = lax.optimization_barrier((own_top, own_end, other))
    m_end, p_top = along_y(own_end, 1), along_y(own_top, -1)
    far_top, far_end = along_y(m_top, 1), along_y(p_end, -1)
    other_m, other_p = along_y(other, 1), along_y(other, -1)
    other_far = across_z(jnp.concatenate([far_top, far_end], axis=0))

    down = adapter_down_maps
    kv_weights, kv_ups = (key_weight, value_weight), (key_up_maps, value_up_maps)
    rows1 = [own, m_top, p_end, far_top, far_end, other]
    rows2 = [m_end, p_top, other_m, other_p, other_far]
    kv = project(info, rows1, CHUNKS[:HALF_CHUNKS], down, (1, 2), kv_weights, kv_ups)
    q_operands = (down, (0,), (query_weight,), (query_up_maps,))
    q1 = project(info, rows1, CHUNKS[:HALF_CHUNKS], *q_operands)
    kv, q1 = lax.optimization_barrier((kv, q1))
    kv = project(info, rows2, CHUNKS[HALF_CHUNKS:], down, (1, 2), kv_weights, kv_ups, before=(kv,))
    steps = flipped(kv, 2), along_x(kv, 1), along_x(kv, -1), along_x(kv, 2)
    q2 = project(info, rows2, CHUNKS[HALF_CHUNKS:], *q_operands)
    other, q2 = lax.optimization_barrier((steps[0], q2))
    steps = (other, *steps[1:])
    shares = both_cores(in_steps(kv, *steps))
    queries = (q1, q2)

    def products(mixed, bases, halved=()):
        weights = output_weight, output_down_maps, output_up_maps
        return output(info, mixed, *weights, bases, halved)

    mixed, kv = attend(info, queries, ((7, 5, 6),), shares)
    bf, bm, bp = products(mixed, (7, 5, 6))
    for_far, from_m, from_p = across_z(bf), along_y(bp, 1), along_y(bm, -1)
    mixed = attend(info, queries, ((3, 1, 2), (4,)), kv=kv)
    af, am_top, am_end, ap_top, ap_end, b0 = products(mixed, (3, 1, 2, 4), halved=(1, 2))
    from_m_end, from_p_top = along_y(ap_end, 1), along_y(am_top, -1)
    far = added(af, for_far)
    other_sum = added(b0, from_m, from_p)
    queries, far, other_sum = lax.optimization_barrier((queries, far, other_sum))
    top, end = along_y(far[:mid], 1), along_y(far[mid:], -1)
    for_own = across_z(other_sum)
    to_p, to_m = added(ap_top, top), added(am_end, end)
    from_m_top, from_p_end = along_y(to_p, 1), along_y(to_m, -1)
    (a0,) = products(attend(info, queries, ((0,),), kv=kv), (0,))
    late = jnp.concatenate([from_m_top, from_p_end], axis=0)
    early = jnp.concatenate([from_p_top, from_m_end], axis=0)
    return added(late, early, for_own, a0)


def solution(mesh):
    return jax.shard_map(
        shards,
        mesh=mesh,
        in_specs=(
            P(("blk", "uly"), None),
            P(),
            P(None, "uly"),
            P(None, "uly"),
            P(None, "uly"),
            P("uly", None),
            P(),
            P(None, "uly"),
            P(None, "uly"),
            P(None, "uly"),
            P("uly", None),
            P(),
            P(),
            P(),
        ),
        out_specs=P(("blk", "uly"), None),
        check_vma=False,
    )
```
